32 devices in a mesh: row: 4 (over y, core), col: 8 (over z, x).
Axes of the slice: x: 2, y: 2, z: 4, core: 2. Of those that a mesh axis runs over, the one named last changes fastest.
Arguments:
- mock_maps: bfloat16 [512, 40960], P('col', 'row'), may hold values from -6 to 6
- window_blocks: int32 [4], replicated, may hold values from 0 to 31, as said below
- kept_tiles: int32 [32, 4], P(('row', 'col')), may hold values from 0 to 1, as said below
- taper_index: int32 [32, 4], P(('row', 'col')), may hold values from 0 to 3, as said below
- taper_table: float32 [4], replicated, may hold values from 0.25 to 2
Outputs:
- covariance: bfloat16 [40960, 5120], P(('row', 'col'))
The draws below stay inside these ranges and needn't reach their ends.
Inputs may be any that keep to these rules, and one draw needn't show every extreme that they name: `window_blocks`: the entries are distinct feature blocks; the first and the last feature block are always among them. `kept_tiles`: A tile whose row block is its own window column block is always kept. `taper_index`: A tile whose row block is its own window column block takes entry 0.
All inputs are finite; a program needn't handle non-finite values.
Results may differ from the reference program's by a relative error of at most 0.001.
Values may be sent and summed in bfloat16 or wider, within the bound.
A program may use at most 128 MiB of HBM per device.

```python
import math
import jax
import jax.numpy as jnp
from jax import lax

FB = 1280
WINDOW = 4
NSEP = 4
MOCKS = 512
NBLK = 32
FEATURES = 40960


def layout_draw(key):
    middle = (jax.random.permutation(jax.random.fold_in(key, 13), NBLK - 2)[:WINDOW - 2] + 1).astype(jnp.int32)
    ends = jnp.array([0, NBLK - 1], dtype=jnp.int32)
    chosen = jnp.concatenate([ends, middle]).astype(jnp.int32)
    order = jax.random.permutation(jax.random.fold_in(key, 14), WINDOW)
    window_ids = chosen[order].astype(jnp.int32)
    separation = jax.random.randint(jax.random.fold_in(key, 12), (NBLK, WINDOW), 0, 2 * NSEP).astype(jnp.int32)
    row_ids = jnp.arange(NBLK, dtype=jnp.int32)[:, None]
    separation = jnp.where(row_ids == window_ids[None, :], 0, separation).astype(jnp.int32)
    return (window_ids, separation)


def draw_window_blocks(key, part):
    return layout_draw(key)[0]


def draw_kept_tiles(key, part):
    return (layout_draw(key)[1] < NSEP).astype(jnp.int32)


def draw_taper_index(key, part):
    return (layout_draw(key)[1] % NSEP).astype(jnp.int32)


def block_levels(stream_key, extent, split, least, high):
    loudness = 1.0
    for position, shards_of in split:
        heights = jax.random.uniform(jax.random.fold_in(jax.random.fold_in(stream_key, 6), position), (shards_of,), jnp.float32, least / len(split), high / len(split))
        loudness = loudness * jnp.repeat(jnp.exp(heights), extent[position] // shards_of).reshape((-1,) + (1,) * (len(extent) - 1 - position))
    return loudness


def scatter_about(own_key, extent, width, most, pieces=(), kind=jnp.bfloat16):
    entries = jax.random.normal(own_key, extent, jnp.float32) * width
    if len(pieces) > 0:
        entries = block_levels(own_key, extent, pieces, -0.22, 0.18) * entries
    return jnp.clip(entries, min=-most, max=most).astype(kind)


def setup_inputs(seed: int = 0) -> dict:
    seeds = jax.random.split(jax.random.key(seed), 6)
    mock_maps = scatter_about(seeds[0], (MOCKS, FEATURES), 1.0, 6.0, ((0, 8), (1, 4)))
    window_blocks = draw_window_blocks(jax.random.fold_in(seeds[5], 71), 0)
    kept_tiles = draw_kept_tiles(jax.random.fold_in(seeds[5], 71), 0)
    taper_index = draw_taper_index(jax.random.fold_in(seeds[5], 71), 0)
    taper_table = jnp.clip(jnp.exp(jax.random.uniform(seeds[4], (NSEP,), jnp.float32, math.log(0.25), math.log(2.0))), 0.25, 2.0)
    return dict(mock_maps=mock_maps, window_blocks=window_blocks, kept_tiles=kept_tiles, taper_index=taper_index, taper_table=taper_table)


def reference(mock_maps, window_blocks, kept_tiles, taper_index, taper_table):
    mock_count = mock_maps.shape[0]
    mean_all = jnp.sum(mock_maps, axis=0, dtype=jnp.float32) / mock_count
    panel_list = []
    panel_means = []
    for slot in range(WINDOW):
        start = (window_blocks[slot] * FB).astype(jnp.int32)
        panel_list.append(lax.dynamic_slice_in_dim(mock_maps, start, FB, 1).astype(jnp.float32))
        panel_means.append(lax.dynamic_slice_in_dim(mean_all, start, FB, 0))
    panels = jnp.concatenate(panel_list, axis=1)
    panel_mean = jnp.concatenate(panel_means, axis=0)

    def one_block(block_id):
        start = (block_id * FB).astype(jnp.int32)
        rows = lax.dynamic_slice_in_dim(mock_maps, start, FB, 1).astype(jnp.float32)
        row_mean = lax.dynamic_slice_in_dim(mean_all, start, FB, 0)
        products = jnp.dot(rows.T, panels, precision=lax.Precision.HIGHEST)
        weights = taper_table[taper_index[block_id]]
        keep = kept_tiles[block_id]
        weight_cols = jnp.repeat(weights, FB)
        keep_cols = jnp.repeat(keep, FB)
        centred = products - mock_count * row_mean[:, None] * panel_mean[None, :]
        tile_value = weight_cols[None, :] * centred / (mock_count - 1)
        tile_value = jnp.where(keep_cols[None, :] > 0, tile_value, jnp.float32(0.0))
        return tile_value.astype(jnp.bfloat16)

    tiles = lax.map(one_block, jnp.arange(NBLK, dtype=jnp.int32))
    return tiles.reshape(NBLK * FB, WINDOW * FB)
```

```python
import functools

import jax
import jax.numpy as jnp
from jax import lax
from jax.experimental import pallas as pl
from jax.experimental.pallas import tpu as pltpu
from jax.sharding import PartitionSpec as P

MESH = pl.DeviceIdType.MESH
WINDOW = 4
CORES = 2
ALONG_Z = 4


def window_kernel(row_count, col_count, window_ref, maps_ref, held_ref):
    row = lax.axis_index("row")
    width = maps_ref.shape[1] // col_count
    part = held_ref.shape[3]
    for r in range(row_count):
        first = r * part
        block = window_ref[first // width]
        start = pl.multiple_of(lax.rem(block, col_count) * width + first % width, 128)
        here = lax.div(block, col_count) == row

        @pl.when(here)
        def _():
            held_ref[r % CORES, r // CORES] = maps_ref[:, pl.ds(start, part)]

        @pl.when(jnp.logical_not(here))
        def _():
            held_ref[r % CORES, r // CORES] = jnp.zeros(held_ref.shape[2:], held_ref.dtype)


def gather_kernel(
    row_count, col_count, held_ref, maps_ref, own_ref, panels_ref,
    from_twin, summed, from_y, piece,
    twin_send, twin_recv, ysum_send, ysum_recv,
    z_send, x_send, y_send, core_send, panel_recv,
    own_send, own_recv, local_sem,
):
    ny, nx, nz = row_count // CORES, col_count // ALONG_Z, ALONG_Z
    row, col = lax.axis_index("row"), lax.axis_index("col")
    y, core = row // CORES, row % CORES
    z, x = col // nx, col % nx
    twin = y * CORES + (1 - core)
    width = own_ref.shape[2]
    part = panels_ref.shape[3]

    def row_of(d):
        return lax.rem(y + d, ny) * CORES + core

    barrier = pltpu.get_barrier_semaphore()
    peers = [(row, lax.rem(col + d, col_count)) for d in range(1, col_count)]
    peers += [(twin, col)] + [(row_of(d), col) for d in range(1, ny)]
    for peer in peers:
        pl.semaphore_signal(barrier, inc=1, device_id=peer, device_id_type=MESH)

    pl.semaphore_wait(barrier, len(peers))

    started = []

    def send(src, dst, send_sem, recv_sem, device):
        copy = pltpu.make_async_remote_copy(
            src_ref=src, dst_ref=dst, send_sem=send_sem, recv_sem=recv_sem,
            device_id=device, device_id_type=MESH,
        )
        copy.start()
        return copy

    def send_own(d):
        dest = lax.rem(col + d, col_count)
        columns = pl.ds(pl.multiple_of(dest * width, 128), width)
        started.append(send(
            maps_ref.at[:, columns], own_ref.at[col],
            own_send.at[d], own_recv.at[col], (row, dest),
        ))

    pending = list(range(1, col_count))
    pending.sort(key=lambda d: -abs(d - col_count // 2))
    pending = pending[::-1]

    def send_some(count):
        for _ in range(min(count, len(pending))):
            send_own(pending.pop(0))

    twin_copy = send(held_ref.at[1 - core], from_twin, twin_send, twin_recv, (twin, col))
    keep_own = pltpu.make_async_copy(
        maps_ref.at[:, pl.ds(pl.multiple_of(col * width, 128), width)], own_ref.at[col], local_sem.at[0]
    )
    keep_own.start()
    twin_copy.wait_recv()
    for d in range(ny):
        part_y = lax.rem(y + d, ny)
        summed[d] = held_ref[core, part_y] + from_twin[part_y]
    for d in range(1, ny):
        started.append(send(
            summed.at[d], from_y.at[ny - d], ysum_send.at[d], ysum_recv.at[ny - d], (row_of(d), col)
        ))
    send_some(2)
    total = summed[0]
    for d in range(1, ny):
        pltpu.make_async_remote_copy(
            src_ref=summed.at[d], dst_ref=from_y.at[d], send_sem=ysum_send.at[d],
            recv_sem=ysum_recv.at[d], device_id=(row, col), device_id_type=MESH,
        ).wait_recv()
        total = total + from_y[d]
    piece[...] = total
    keep_piece = pltpu.make_async_copy(piece, panels_ref.at[row, col], local_sem.at[1])
    keep_piece.start()

    def slot(r, c):
        return panels_ref.at[r, c]

    def arrived(r, c):
        pltpu.make_async_remote_copy(
            src_ref=slot(r, c), dst_ref=slot(r, c), send_sem=core_send.at[r, c],
            recv_sem=panel_recv.at[r, c], device_id=(row, col), device_id_type=MESH,
        ).wait_recv()

    def out(src, r, c, send_sem, device, waiting):
        copy = pltpu.make_async_remote_copy(
            src_ref=src, dst_ref=slot(r, c), send_sem=send_sem,
            recv_sem=panel_recv.at[r, c], device_id=device, device_id_type=MESH,
        )
        if waiting:
            copy.wait_send()
        else:
            copy.start()

    def z_out(src, zz, up, waiting):
        to = z + 1 if up else z - 1

        @pl.when(to < nz if up else to >= 0)
        def _():
            c = zz * nx + x
            out(src, row, c, z_send.at[int(up), zz], (row, to * nx + x), waiting)

    def x_out(src, zz, waiting):
        c = zz * nx + x
        for d in range(1, nx):
            out(src, row, c, x_send.at[d, zz], (row, z * nx + lax.rem(x + d, nx)), waiting)

    def y_out(src, c, waiting):
        for d in range(1, ny):
            out(src, row, c, y_send.at[d, c], (row_of(d), col), waiting)

    def core_out(src, r, c, waiting):
        out(src, r, c, core_send.at[r, c], (twin, col), waiting)

    def at_z(d, body):
        if d == 0:
            body(z, None)
            return

        @pl.when(z >= d)
        def _():
            body(z - d, True)

        @pl.when(z + d < nz)
        def _():
            body(z + d, False)

    def z_event(waiting, zz, up):
        c = zz * nx + x
        if up is None:
            src = piece
            z_out(src, zz, True, waiting)
            z_out(src, zz, False, waiting)
        else:
            src = slot(row, c)
            if not waiting:
                arrived(row, c)
            z_out(src, zz, up, waiting)
        y_out(src, c, waiting)
        x_out(src, zz, waiting)
        core_out(src, row, c, waiting)

    def x_event(waiting, zz, up):
        for d in range(1, nx):
            c = zz * nx + lax.rem(x + d, nx)
            if not waiting:
                arrived(row, c)
            y_out(slot(row, c), c, waiting)
            core_out(slot(row, c), row, c, waiting)

    def y_event(waiting, own_x, zz, up):
        for dx in ([0] if own_x else range(1, nx)):
            c = zz * nx + lax.rem(x + dx, nx)
            for d in range(1, ny):
                r = row_of(d)
                if not waiting:
                    arrived(r, c)
                core_out(slot(r, c), r, c, waiting)

    def events(waiting):
        at_z(0, functools.partial(z_event, waiting))
        if not waiting:
            send_some(2)
        for d in range(1, nz):
            at_z(d, functools.partial(z_event, waiting))
            at_z(d - 1, functools.partial(x_event, waiting))
            if not waiting:
                send_some(1 if d < nz - 1 else col_count)
        at_z(nz - 1, functools.partial(x_event, waiting))
        for d in range(nz):
            at_z(d, functools.partial(y_event, waiting, True))
            at_z(d, functools.partial(y_event, waiting, False))

    events(False)

    for d in range(ny):
        r = lax.rem(y + d, ny) * CORES + (1 - core)

        @pl.loop(0, col_count)
        def _(c):
            arrived(r, c)

    for d in range(1, col_count):
        source = lax.rem(col + d, col_count)
        pltpu.make_async_remote_copy(
            src_ref=own_ref.at[source], dst_ref=own_ref.at[source], send_sem=own_send.at[d],
            recv_sem=own_recv.at[source], device_id=(row, source), device_id_type=MESH,
        ).wait_recv()
    twin_copy.wait_send()
    for copy in started:
        copy.wait_send()
    events(True)
    keep_own.wait()
    keep_piece.wait()


def gather(mock_maps, window_blocks, row_count, col_count):
    mocks = mock_maps.shape[0]
    width = mock_maps.shape[1] // col_count
    part = WINDOW * width // row_count
    ny = row_count // CORES
    nx = col_count // ALONG_Z
    dma = pltpu.SemaphoreType.DMA
    vmem = pl.BlockSpec(memory_space=pltpu.VMEM)
    held = pl.pallas_call(
        functools.partial(window_kernel, row_count, col_count),
        out_shape=jax.ShapeDtypeStruct((CORES, ny, mocks, part), jnp.bfloat16),
        in_specs=[pl.BlockSpec(memory_space=pltpu.SMEM), vmem],
        out_specs=vmem,
        name="window",
    )(window_blocks, mock_maps)
    return pl.pallas_call(
        functools.partial(gather_kernel, row_count, col_count),
        out_shape=(
            jax.ShapeDtypeStruct((col_count, mocks, width), jnp.bfloat16),
            jax.ShapeDtypeStruct((row_count, col_count, mocks, part), jnp.bfloat16),
        ),
        in_specs=[vmem, vmem],
        out_specs=(pl.BlockSpec(memory_space=pl.ANY), pl.BlockSpec(memory_space=pl.ANY)),
        scratch_shapes=[
            pltpu.VMEM((ny, mocks, part), jnp.bfloat16),
            pltpu.VMEM((ny, mocks, part), jnp.bfloat16),
            pltpu.VMEM((ny, mocks, part), jnp.bfloat16),
            pltpu.VMEM((mocks, part), jnp.bfloat16),
            dma, dma, dma((ny,)), dma((ny,)),
            dma((2, ALONG_Z)), dma((nx, ALONG_Z)), dma((ny, col_count)),
            dma((row_count, col_count)), dma((row_count, col_count)),
            dma((col_count,)), dma((col_count,)), dma((2,)),
        ],
        compiler_params=pltpu.CompilerParams(
            collective_id=0, has_side_effects=True, vmem_limit_bytes=32 * 2**20
        ),
        name="gather",
    )(held, mock_maps)


def tile_kernel(chunks_per_block, kept_ref, index_ref, table_ref, own_ref, panel_ref, out_ref, own_t, own_sum):
    step = pl.program_id(0)
    slot = step // chunks_per_block
    count, width = own_ref.shape

    @pl.when(step == 0)
    def _():
        own_t[...] = own_ref[...].T
        own_sum[...] = jnp.dot(
            own_t[...], jnp.ones((count, 128), jnp.bfloat16), preferred_element_type=jnp.float32
        )

    kept = kept_ref[0, slot] > 0

    @pl.when(kept)
    def _():
        panel = panel_ref[0]
        scale = table_ref[index_ref[0, slot]] / (count - 1)
        panel_mean = jnp.sum(panel.astype(jnp.float32), axis=0, keepdims=True) / count
        rows = 256
        for first in range(0, width, rows):
            here = slice(first, min(first + rows, width))
            products = jnp.dot(own_t[here, :], panel, preferred_element_type=jnp.float32)
            centred = products - own_sum[here, :1] * panel_mean
            out_ref[here, :] = (scale * centred).astype(jnp.bfloat16)

    @pl.when(jnp.logical_not(kept))
    def _():
        out_ref[...] = jnp.zeros_like(out_ref)


def tiles(own, panels, kept_tiles, taper_index, taper_table):
    count, width = own.shape
    parts, _, part = panels.shape
    chunk = part if part <= 640 else 640
    per_part = part // chunk
    smem = pl.BlockSpec(memory_space=pltpu.SMEM)
    steps = parts * per_part
    return pl.pallas_call(
        functools.partial(tile_kernel, width // chunk),
        grid=(steps,),
        out_shape=jax.ShapeDtypeStruct((width, parts * part), jnp.bfloat16),
        in_specs=[
            smem, smem, smem,
            pl.BlockSpec((count, width), lambda i: (0, 0)),
            pl.BlockSpec((1, count, chunk), lambda i: (i // per_part, 0, i % per_part)),
        ],
        out_specs=pl.BlockSpec((width, chunk), lambda i: (0, i)),
        scratch_shapes=[
            pltpu.VMEM((width, count), jnp.bfloat16),
            pltpu.VMEM((width, 128), jnp.float32),
        ],
        compiler_params=pltpu.CompilerParams(
            dimension_semantics=("arbitrary",), vmem_limit_bytes=40 * 2**20
        ),
        name="tiles",
    )(kept_tiles, taper_index, taper_table, own, panels)


def per_device(row_count, col_count, mock_maps, window_blocks, kept_tiles, taper_index, taper_table):
    own, panels = gather(mock_maps, window_blocks, row_count, col_count)
    own = own.reshape(-1, own.shape[-1])
    panels = panels.reshape(panels.shape[0], -1, panels.shape[-1])
    return tiles(own, panels, kept_tiles, taper_index, taper_table)


def solution(mesh):
    in_specs = (P("col", "row"), P(), P(("row", "col"), None), P(("row", "col"), None), P())
    out_specs = P(("row", "col"), None)
    return jax.shard_map(
        functools.partial(per_device, mesh.shape["row"], mesh.shape["col"]),
        mesh=mesh, in_specs=in_specs, out_specs=out_specs, check_vma=False,
    )
```

```python
import functools

import jax
import jax.numpy as jnp
from jax import lax
from jax.experimental import pallas as pl
from jax.experimental.pallas import tpu as pltpu
from jax.sharding import PartitionSpec as P

MESH = pl.DeviceIdType.MESH
WINDOW = 4
CORES = 2
ALONG_Z = 4


def gather_kernel(
    row_count, col_count, window_ref, maps_ref, own_ref, panels_ref,
    maps, for_twin, mine, from_twin, summed, from_y, piece,
    twin_send, twin_recv, ysum_send, ysum_recv,
    z_send, x_send, y_send, core_send, panel_recv,
    own_send, own_recv, local_sem,
):
    ny, nx, nz = row_count // CORES, col_count // ALONG_Z, ALONG_Z
    row, col = lax.axis_index("row"), lax.axis_index("col")
    y, core = row // CORES, row % CORES
    z, x = col // nx, col % nx
    twin = y * CORES + (1 - core)
    width = own_ref.shape[2]
    part = panels_ref.shape[3]

    load_maps = pltpu.make_async_copy(maps_ref, maps, local_sem.at[2])
    load_maps.start()

    def row_of(d):
        return lax.rem(y + d, ny) * CORES + core

    barrier = pltpu.get_barrier_semaphore()
    peers = [(row, lax.rem(col + d, col_count)) for d in range(1, col_count)]
    peers += [(twin, col)] + [(row_of(d), col) for d in range(1, ny)]
    for peer in peers:
        pl.semaphore_signal(barrier, inc=1, device_id=peer, device_id_type=MESH)

    last = row_count * col_count - 1
    is_middle, rank, seen = [], [], 0
    for t in range(WINDOW):
        block = window_ref[t]
        is_middle.append(jnp.minimum(block, 1) * jnp.minimum(last - block, 1))
        rank.append(seen)
        seen = seen + is_middle[t]

    def masked(slot, offset):
        block = jnp.int32(0)
        for t in range(WINDOW):
            chosen = is_middle[t] * (1 - jnp.minimum(jnp.abs(rank[t] + 1 - slot), 1))
            block = block + chosen * window_ref[t]
        block = block + last * (1 - jnp.minimum(jnp.abs(slot - (WINDOW - 1)), 1))
        found = jnp.zeros((maps.shape[0], part), jnp.float32)
        for j in range(col_count):
            here = 1 - jnp.minimum(jnp.abs(block - (row * col_count + j)), 1)
            columns = maps[:, pl.ds(pl.multiple_of(j * width + offset, 128), part)]
            found = found + columns.astype(jnp.float32) * here.astype(jnp.float32)
        return found.astype(jnp.bfloat16)

    pl.semaphore_wait(barrier, len(peers))

    started = []

    def send(src, dst, send_sem, recv_sem, device):
        copy = pltpu.make_async_remote_copy(
            src_ref=src, dst_ref=dst, send_sem=send_sem, recv_sem=recv_sem,
            device_id=device, device_id_type=MESH,
        )
        copy.start()
        return copy

    def send_own(d):
        dest = lax.rem(col + d, col_count)
        columns = pl.ds(pl.multiple_of(dest * width, 128), width)
        started.append(send(
            maps_ref.at[:, columns], own_ref.at[col],
            own_send.at[d], own_recv.at[col], (row, dest),
        ))

    pending = list(range(1, col_count))
    pending.sort(key=lambda d: -abs(d - col_count // 2))
    pending = pending[::-1]

    def send_some(count):
        for _ in range(min(count, len(pending))):
            send_own(pending.pop(0))

    def slot(r, c):
        return panels_ref.at[r, c]

    def arrived(r, c):
        pltpu.make_async_remote_copy(
            src_ref=slot(r, c), dst_ref=slot(r, c), send_sem=core_send.at[r, c],
            recv_sem=panel_recv.at[r, c], device_id=(row, col), device_id_type=MESH,
        ).wait_recv()

    def out(src, r, c, send_sem, device, waiting):
        copy = pltpu.make_async_remote_copy(
            src_ref=src, dst_ref=slot(r, c), send_sem=send_sem,
            recv_sem=panel_recv.at[r, c], device_id=device, device_id_type=MESH,
        )
        if waiting:
            copy.wait_send()
        else:
            copy.start()

    def z_out(src, zz, up, waiting):
        to = z + 1 if up else z - 1

        @pl.when(to < nz if up else to >= 0)
        def _():
            c = zz * nx + x
            out(src, row, c, z_send.at[int(up), zz], (row, to * nx + x), waiting)

    def x_out(src, zz, waiting):
        c = zz * nx + x
        for d in range(1, nx):
            out(src, row, c, x_send.at[d, zz], (row, z * nx + lax.rem(x + d, nx)), waiting)

    def y_out(src, c, waiting):
        for d in range(1, ny):
            out(src, row, c, y_send.at[d, c], (row_of(d), col), waiting)

    def core_out(src, r, c, waiting):
        out(src, r, c, core_send.at[r, c], (twin, col), waiting)

    def at_z(d, body):
        if d == 0:
            body(z, None)
            return

        @pl.when(z >= d)
        def _():
            body(z - d, True)

        @pl.when(z + d < nz)
        def _():
            body(z + d, False)

    def own_event(src, waiting):
        z_out(src, z, True, waiting)
        z_out(src, z, False, waiting)
        y_out(src, col, waiting)
        x_out(src, z, waiting)
        core_out(src, row, col, waiting)

    def z_event(waiting, zz, up):
        c = zz * nx + x
        src = slot(row, c)
        if not waiting:
            arrived(row, c)
        z_out(src, zz, up, waiting)
        y_out(src, c, waiting)
        x_out(src, zz, waiting)
        core_out(src, row, c, waiting)

    def x_event(waiting, zz, up):
        for d in range(1, nx):
            c = zz * nx + lax.rem(x + d, nx)
            if not waiting:
                arrived(row, c)
            y_out(slot(row, c), c, waiting)
            core_out(slot(row, c), row, c, waiting)

    def y_event(waiting, own_x, zz, up):
        for dx in ([0] if own_x else range(1, nx)):
            c = zz * nx + lax.rem(x + dx, nx)
            for d in range(1, ny):
                r = row_of(d)
                if not waiting:
                    arrived(r, c)
                core_out(slot(r, c), r, c, waiting)

    def events(waiting):
        if waiting:
            own_event(piece, True)
        for d in range(1, nz):
            at_z(d, functools.partial(z_event, waiting))
            at_z(d - 1, functools.partial(x_event, waiting))
            if not waiting:
                send_some(2 if d < nz - 2 else col_count)
        at_z(nz - 1, functools.partial(x_event, waiting))
        for d in range(nz):
            at_z(d, functools.partial(y_event, waiting, True))
            at_z(d, functools.partial(y_event, waiting, False))

    keep_own = pltpu.make_async_copy(
        maps_ref.at[:, pl.ds(pl.multiple_of(col * width, 128), width)], own_ref.at[col], local_sem.at[0]
    )
    keep_own.start()
    direct = part == width and row_count == WINDOW
    ends = lax.rem(row, row_count - 1) == 0

    def y_sum(d):
        return pltpu.make_async_remote_copy(
            src_ref=summed.at[d], dst_ref=from_y.at[ny - d], send_sem=ysum_send.at[d],
            recv_sem=ysum_recv.at[ny - d], device_id=(row_of(d), col), device_id_type=MESH,
        )

    if direct:
        first = pl.multiple_of((row // (row_count - 1)) * ((col_count - 1) * width), 128)
        held_piece = maps_ref.at[:, pl.ds(first, width)]

        @pl.when(ends)
        def _():
            own_event(held_piece, False)
            pltpu.make_async_copy(held_piece, slot(row, col), local_sem.at[1]).start()

        send_some(2)
        load_maps.wait()
        for_twin[0] = masked(1 + core, 0)
        mine[0] = masked(2 - core, 0)
        twin_copy = send(for_twin, from_twin, twin_send, twin_recv, (twin, col))
        twin_copy.wait_recv()
        summed[1] = mine[0] + from_twin[0]

        @pl.when(ends)
        def _():
            y_sum(1).start()

        @pl.when(jnp.logical_not(ends))
        def _():
            y_sum(1).wait_recv()
            piece[...] = summed[1] + from_y[1]
            own_event(piece, False)
            pltpu.make_async_copy(piece, slot(row, col), local_sem.at[1]).start()
    else:
        load_maps.wait()
        for d in range(ny):
            for k, held in ((1 - core, for_twin), (core, mine)):
                first = (lax.rem(y + d, ny) * CORES + k) * part
                held[d] = masked(first // width, lax.rem(first, width))
        twin_copy = send(for_twin, from_twin, twin_send, twin_recv, (twin, col))
        twin_copy.wait_recv()
        for d in range(ny):
            summed[d] = mine[d] + from_twin[d]
        for d in range(1, ny):
            y_sum(d).start()
        send_some(2)
        total = summed[0]
        for d in range(1, ny):
            y_sum(d).wait_recv()
            total = total + from_y[ny - d]
        piece[...] = total
        own_event(piece, False)
        pltpu.make_async_copy(piece, slot(row, col), local_sem.at[1]).start()
    send_some(2)
    events(False)

    for d in range(ny):
        r = lax.rem(y + d, ny) * CORES + (1 - core)

        @pl.loop(0, col_count)
        def _(c):
            arrived(r, c)

    for d in range(1, col_count):
        source = lax.rem(col + d, col_count)
        pltpu.make_async_remote_copy(
            src_ref=own_ref.at[source], dst_ref=own_ref.at[source], send_sem=own_send.at[d],
            recv_sem=own_recv.at[source], device_id=(row, source), device_id_type=MESH,
        ).wait_recv()
    twin_copy.wait_send()
    for copy in started:
        copy.wait_send()
    if direct:
        @pl.when(ends)
        def _():
            y_sum(1).wait_send()
    else:
        for d in range(1, ny):
            y_sum(d).wait_send()
    events(True)
    keep_own.wait()
    pltpu.make_async_copy(piece, slot(row, col), local_sem.at[1]).wait()


def gather(mock_maps, window_blocks, row_count, col_count):
    mocks = mock_maps.shape[0]
    width = mock_maps.shape[1] // col_count
    part = WINDOW * width // row_count
    ny = row_count // CORES
    nx = col_count // ALONG_Z
    dma = pltpu.SemaphoreType.DMA
    shares = 1 if part == width else ny
    return pl.pallas_call(
        functools.partial(gather_kernel, row_count, col_count),
        out_shape=(
            jax.ShapeDtypeStruct((col_count, mocks, width), jnp.bfloat16),
            jax.ShapeDtypeStruct((row_count, col_count, mocks, part), jnp.bfloat16),
        ),
        in_specs=[pl.BlockSpec(memory_space=pltpu.SMEM), pl.BlockSpec(memory_space=pl.ANY)],
        out_specs=(pl.BlockSpec(memory_space=pl.ANY), pl.BlockSpec(memory_space=pl.ANY)),
        scratch_shapes=[
            pltpu.VMEM(mock_maps.shape, jnp.bfloat16),
            pltpu.VMEM((shares, mocks, part), jnp.bfloat16),
            pltpu.VMEM((shares, mocks, part), jnp.bfloat16),
            pltpu.VMEM((shares, mocks, part), jnp.bfloat16),
            pltpu.VMEM((ny, mocks, part), jnp.bfloat16),
            pltpu.VMEM((ny, mocks, part), jnp.bfloat16),
            pltpu.VMEM((mocks, part), jnp.bfloat16),
            dma, dma, dma((ny,)), dma((ny,)),
            dma((2, ALONG_Z)), dma((nx, ALONG_Z)), dma((ny, col_count)),
            dma((row_count, col_count)), dma((row_count, col_count)),
            dma((col_count,)), dma((col_count,)), dma((3,)),
        ],
        compiler_params=pltpu.CompilerParams(
            collective_id=0, has_side_effects=True, vmem_limit_bytes=60 * 2**20
        ),
        name="gather",
    )(window_blocks, mock_maps)


def ordered_slot(window_ref, last, slot):
    block = window_ref[slot]
    rank = jnp.int32(1)
    for t in range(WINDOW):
        middle = (t < slot) & (window_ref[t] != 0) & (window_ref[t] != last)
        rank = rank + middle.astype(jnp.int32)
    return jnp.where(block == 0, 0, jnp.where(block == last, WINDOW - 1, rank))


ONES = 16
HALVES = 2


def tile_kernel(parts, window_ref, kept_ref, index_ref, table_ref, own_ref, panel_ref, out_ref, own_t):
    step, half = pl.program_id(0), pl.program_id(1)
    slot = step // parts
    count, width = own_ref.shape
    rows = width // HALVES

    @pl.when((step == 0) & (half == 0))
    def _():
        for h in range(HALVES):
            own_t[h, :ONES] = jnp.ones((ONES, count), jnp.bfloat16)
            own_t[h, ONES:] = own_ref[:, h * rows:(h + 1) * rows].T

    kept = kept_ref[0, slot] > 0

    @pl.when(kept)
    def _():
        scale = table_ref[index_ref[0, slot]] / (count - 1)
        own_sum = jnp.dot(
            own_t[half, ONES:], jnp.ones((count, 128), jnp.bfloat16), preferred_element_type=jnp.float32
        )
        for first in range(0, out_ref.shape[1], 256):
            panel = panel_ref[0, :, first:first + 256]
            products = jnp.dot(own_t[half], panel, preferred_element_type=jnp.float32)
            panel_mean = products[:1] / count
            for part in range(0, panel.shape[1], 128):
                here = slice(part, part + 128)
                centred = products[ONES:, here] - own_sum * panel_mean[:, here]
                out_ref[:, first + part:first + part + 128] = (scale * centred).astype(jnp.bfloat16)

    @pl.when(jnp.logical_not(kept))
    def _():
        out_ref[...] = jnp.zeros_like(out_ref)


def tiles(own, panels, window_blocks, kept_tiles, taper_index, taper_table, last):
    count, width = own.shape
    steps, _, part = panels.shape
    parts = width // part
    smem = pl.BlockSpec(memory_space=pltpu.SMEM)

    def panel_index(i, h, window_ref):
        return ordered_slot(window_ref, last, i // parts) * parts + i % parts, 0, 0

    return pl.pallas_call(
        functools.partial(tile_kernel, parts),
        out_shape=jax.ShapeDtypeStruct((width, steps * part), jnp.bfloat16),
        grid_spec=pltpu.PrefetchScalarGridSpec(
            num_scalar_prefetch=1,
            grid=(steps, HALVES),
            in_specs=[
                smem, smem, smem,
                pl.BlockSpec((count, width), lambda i, h, w: (0, 0)),
                pl.BlockSpec((1, count, part), panel_index),
            ],
            out_specs=pl.BlockSpec((width // HALVES, part), lambda i, h, w: (h, i)),
            scratch_shapes=[pltpu.VMEM((HALVES, ONES + width // HALVES, count), jnp.bfloat16)],
        ),
        compiler_params=pltpu.CompilerParams(
            dimension_semantics=("arbitrary", "arbitrary"), vmem_limit_bytes=60 * 2**20
        ),
        name="tiles",
    )(window_blocks, kept_tiles, taper_index, taper_table, own, panels)


def per_device(row_count, col_count, mock_maps, window_blocks, kept_tiles, taper_index, taper_table):
    own, panels = gather(mock_maps, window_blocks, row_count, col_count)
    own = own.reshape(-1, own.shape[-1])
    panels = panels.reshape(panels.shape[0], -1, panels.shape[-1])
    last = row_count * col_count - 1
    return tiles(own, panels, window_blocks, kept_tiles, taper_index, taper_table, last)


def solution(mesh):
    in_specs = (P("col", "row"), P(), P(("row", "col"), None), P(("row", "col"), None), P())
    out_specs = P(("row", "col"), None)
    return jax.shard_map(
        functools.partial(per_device, mesh.shape["row"], mesh.shape["col"]),
        mesh=mesh, in_specs=in_specs, out_specs=out_specs, check_vma=False,
    )
```

```python
import functools

import jax
import jax.numpy as jnp
from jax import lax
from jax.experimental import pallas as pl
from jax.experimental.pallas import tpu as pltpu
from jax.sharding import PartitionSpec as P

MESH = pl.DeviceIdType.MESH
WINDOW = 4
CORES = 2
ALONG_Z = 4


def gather_kernel(
    row_count, col_count, window_ref, maps_ref, own_ref, panels_ref,
    maps, for_twin, mine, from_twin, summed, from_y, piece,
    twin_send, twin_recv, ysum_send, ysum_recv,
    z_send, x_send, y_send, core_send, panel_recv,
    own_send, own_recv, local_sem,
):
    ny, nx, nz = row_count // CORES, col_count // ALONG_Z, ALONG_Z
    row, col = lax.axis_index("row"), lax.axis_index("col")
    y, core = row // CORES, row % CORES
    z, x = col // nx, col % nx
    twin = y * CORES + (1 - core)
    width = own_ref.shape[2]
    part = panels_ref.shape[3]

    load_maps = pltpu.make_async_copy(maps_ref, maps, local_sem.at[2])
    load_maps.start()

    def row_of(d):
        return lax.rem(y + d, ny) * CORES + core

    barrier = pltpu.get_barrier_semaphore()
    peers = [(row, lax.rem(col + d, col_count)) for d in range(1, col_count)]
    peers += [(twin, col)] + [(row_of(d), col) for d in range(1, ny)]
    for peer in peers:
        pl.semaphore_signal(barrier, inc=1, device_id=peer, device_id_type=MESH)

    last = row_count * col_count - 1
    is_middle, rank, seen = [], [], 0
    for t in range(WINDOW):
        block = window_ref[t]
        is_middle.append(jnp.minimum(block, 1) * jnp.minimum(last - block, 1))
        rank.append(seen)
        seen = seen + is_middle[t]

    def masked(slot, offset):
        block = jnp.int32(0)
        for t in range(WINDOW):
            chosen = is_middle[t] * (1 - jnp.minimum(jnp.abs(rank[t] + 1 - slot), 1))
            block = block + chosen * window_ref[t]
        block = block + last * (1 - jnp.minimum(jnp.abs(slot - (WINDOW - 1)), 1))
        found = jnp.zeros((maps.shape[0], part), jnp.float32)
        for j in range(col_count):
            here = 1 - jnp.minimum(jnp.abs(block - (row * col_count + j)), 1)
            columns = maps[:, pl.ds(pl.multiple_of(j * width + offset, 128), part)]
            found = found + columns.astype(jnp.float32) * here.astype(jnp.float32)
        return found.astype(jnp.bfloat16)

    pl.semaphore_wait(barrier, len(peers))

    started = []

    def send(src, dst, send_sem, recv_sem, device):
        copy = pltpu.make_async_remote_copy(
            src_ref=src, dst_ref=dst, send_sem=send_sem, recv_sem=recv_sem,
            device_id=device, device_id_type=MESH,
        )
        copy.start()
        return copy

    def send_own(d):
        dest = lax.rem(col + d, col_count)
        columns = pl.ds(pl.multiple_of(dest * width, 128), width)
        started.append(send(
            maps_ref.at[:, columns], own_ref.at[col],
            own_send.at[d], own_recv.at[col], (row, dest),
        ))

    pending = list(range(1, col_count))
    pending.sort(key=lambda d: -abs(d - col_count // 2))
    pending = pending[::-1]

    def send_some(count):
        for _ in range(min(count, len(pending))):
            send_own(pending.pop(0))

    def slot(r, c):
        return panels_ref.at[r, c]

    def arrived(r, c):
        pltpu.make_async_remote_copy(
            src_ref=slot(r, c), dst_ref=slot(r, c), send_sem=core_send.at[r, c],
            recv_sem=panel_recv.at[r, c], device_id=(row, col), device_id_type=MESH,
        ).wait_recv()

    def out(src, r, c, send_sem, device, waiting):
        copy = pltpu.make_async_remote_copy(
            src_ref=src, dst_ref=slot(r, c), send_sem=send_sem,
            recv_sem=panel_recv.at[r, c], device_id=device, device_id_type=MESH,
        )
        if waiting:
            copy.wait_send()
        else:
            copy.start()

    def z_out(src, zz, up, waiting):
        to = z + 1 if up else z - 1

        @pl.when(to < nz if up else to >= 0)
        def _():
            c = zz * nx + x
            out(src, row, c, z_send.at[int(up), zz], (row, to * nx + x), waiting)

    def x_out(src, zz, waiting):
        c = zz * nx + x
        for d in range(1, nx):
            out(src, row, c, x_send.at[d, zz], (row, z * nx + lax.rem(x + d, nx)), waiting)

    def y_out(src, c, waiting):
        for d in range(1, ny):
            out(src, row, c, y_send.at[d, c], (row_of(d), col), waiting)

    def core_out(src, r, c, waiting):
        out(src, r, c, core_send.at[r, c], (twin, col), waiting)

    def at_z(d, body):
        if d == 0:
            body(z, None)
            return

        @pl.when(z >= d)
        def _():
            body(z - d, True)

        @pl.when(z + d < nz)
        def _():
            body(z + d, False)

    def own_event(src, waiting):
        z_out(src, z, True, waiting)
        z_out(src, z, False, waiting)
        y_out(src, col, waiting)
        x_out(src, z, waiting)
        core_out(src, row, col, waiting)

    def z_event(waiting, zz, up):
        c = zz * nx + x
        src = slot(row, c)
        if not waiting:
            arrived(row, c)
        z_out(src, zz, up, waiting)
        y_out(src, c, waiting)
        x_out(src, zz, waiting)
        core_out(src, row, c, waiting)

    def x_event(waiting, zz, up):
        for d in range(1, nx):
            c = zz * nx + lax.rem(x + d, nx)
            if not waiting:
                arrived(row, c)
            y_out(slot(row, c), c, waiting)
            core_out(slot(row, c), row, c, waiting)

    def y_event(waiting, own_x, zz, up):
        for dx in ([0] if own_x else range(1, nx)):
            c = zz * nx + lax.rem(x + dx, nx)
            for d in range(1, ny):
                r = row_of(d)
                if not waiting:
                    arrived(r, c)
                core_out(slot(r, c), r, c, waiting)

    def events(waiting):
        if waiting:
            own_event(piece, True)
        for d in range(1, nz):
            at_z(d, functools.partial(z_event, waiting))
            at_z(d - 1, functools.partial(x_event, waiting))
            if not waiting:
                send_some(2 if d < nz - 2 else col_count)
        at_z(nz - 1, functools.partial(x_event, waiting))
        for d in range(nz):
            at_z(d, functools.partial(y_event, waiting, True))
            at_z(d, functools.partial(y_event, waiting, False))

    keep_own = pltpu.make_async_copy(
        maps_ref.at[:, pl.ds(pl.multiple_of(col * width, 128), width)], own_ref.at[col], local_sem.at[0]
    )
    keep_own.start()
    direct = part == width and row_count == WINDOW
    ends = lax.rem(row, row_count - 1) == 0

    def y_sum(d):
        return pltpu.make_async_remote_copy(
            src_ref=summed.at[d], dst_ref=from_y.at[ny - d], send_sem=ysum_send.at[d],
            recv_sem=ysum_recv.at[ny - d], device_id=(row_of(d), col), device_id_type=MESH,
        )

    if direct:
        first = pl.multiple_of((row // (row_count - 1)) * ((col_count - 1) * width), 128)
        held_piece = maps_ref.at[:, pl.ds(first, width)]

        @pl.when(ends)
        def _():
            own_event(held_piece, False)
            pltpu.make_async_copy(held_piece, slot(row, col), local_sem.at[1]).start()

        load_maps.wait()
        for_twin[0] = masked(1 + core, 0)
        mine[0] = masked(2 - core, 0)
        twin_copy = send(for_twin, from_twin, twin_send, twin_recv, (twin, col))
        twin_copy.wait_recv()
        summed[1] = mine[0] + from_twin[0]

        @pl.when(ends)
        def _():
            y_sum(1).start()

        @pl.when(jnp.logical_not(ends))
        def _():
            y_sum(1).wait_recv()
            piece[...] = summed[1] + from_y[1]
            own_event(piece, False)
            pltpu.make_async_copy(piece, slot(row, col), local_sem.at[1]).start()
    else:
        load_maps.wait()
        for d in range(ny):
            for k, held in ((1 - core, for_twin), (core, mine)):
                first = (lax.rem(y + d, ny) * CORES + k) * part
                held[d] = masked(first // width, lax.rem(first, width))
        twin_copy = send(for_twin, from_twin, twin_send, twin_recv, (twin, col))
        twin_copy.wait_recv()
        for d in range(ny):
            summed[d] = mine[d] + from_twin[d]
        for d in range(1, ny):
            y_sum(d).start()
        total = summed[0]
        for d in range(1, ny):
            y_sum(d).wait_recv()
            total = total + from_y[ny - d]
        piece[...] = total
        own_event(piece, False)
        pltpu.make_async_copy(piece, slot(row, col), local_sem.at[1]).start()
    events(False)

    for d in range(ny):
        r = lax.rem(y + d, ny) * CORES + (1 - core)

        @pl.loop(0, col_count)
        def _(c):
            arrived(r, c)

    for d in range(1, col_count):
        source = lax.rem(col + d, col_count)
        pltpu.make_async_remote_copy(
            src_ref=own_ref.at[source], dst_ref=own_ref.at[source], send_sem=own_send.at[d],
            recv_sem=own_recv.at[source], device_id=(row, source), device_id_type=MESH,
        ).wait_recv()
    twin_copy.wait_send()
    for copy in started:
        copy.wait_send()
    if direct:
        @pl.when(ends)
        def _():
            y_sum(1).wait_send()
    else:
        for d in range(1, ny):
            y_sum(d).wait_send()
    events(True)
    keep_own.wait()
    pltpu.make_async_copy(piece, slot(row, col), local_sem.at[1]).wait()


def gather(mock_maps, window_blocks, row_count, col_count):
    mocks = mock_maps.shape[0]
    width = mock_maps.shape[1] // col_count
    part = WINDOW * width // row_count
    ny = row_count // CORES
    nx = col_count // ALONG_Z
    dma = pltpu.SemaphoreType.DMA
    shares = 1 if part == width else ny
    return pl.pallas_call(
        functools.partial(gather_kernel, row_count, col_count),
        out_shape=(
            jax.ShapeDtypeStruct((col_count, mocks, width), jnp.bfloat16),
            jax.ShapeDtypeStruct((row_count, col_count, mocks, part), jnp.bfloat16),
        ),
        in_specs=[pl.BlockSpec(memory_space=pltpu.SMEM), pl.BlockSpec(memory_space=pl.ANY)],
        out_specs=(pl.BlockSpec(memory_space=pl.ANY), pl.BlockSpec(memory_space=pl.ANY)),
        scratch_shapes=[
            pltpu.VMEM(mock_maps.shape, jnp.bfloat16),
            pltpu.VMEM((shares, mocks, part), jnp.bfloat16),
            pltpu.VMEM((shares, mocks, part), jnp.bfloat16),
            pltpu.VMEM((shares, mocks, part), jnp.bfloat16),
            pltpu.VMEM((ny, mocks, part), jnp.bfloat16),
            pltpu.VMEM((ny, mocks, part), jnp.bfloat16),
            pltpu.VMEM((mocks, part), jnp.bfloat16),
            dma, dma, dma((ny,)), dma((ny,)),
            dma((2, ALONG_Z)), dma((nx, ALONG_Z)), dma((ny, col_count)),
            dma((row_count, col_count)), dma((row_count, col_count)),
            dma((col_count,)), dma((col_count,)), dma((3,)),
        ],
        compiler_params=pltpu.CompilerParams(
            collective_id=0, has_side_effects=True, vmem_limit_bytes=60 * 2**20
        ),
        name="gather",
    )(window_blocks, mock_maps)


def ordered_slot(window_ref, last, slot):
    block = window_ref[slot]
    rank = jnp.int32(1)
    for t in range(WINDOW):
        middle = (t < slot) & (window_ref[t] != 0) & (window_ref[t] != last)
        rank = rank + middle.astype(jnp.int32)
    return jnp.where(block == 0, 0, jnp.where(block == last, WINDOW - 1, rank))


ONES = 16
HALVES = 2


def tile_kernel(
    parts, last, window_hbm, kept_hbm, index_hbm, table_hbm, own_hbm, panels_hbm, out_ref,
    window_ref, kept_ref, index_ref, table_ref, own_ref, panels_ref, own_t, small_sem, own_sem, panel_sem,
):
    step, half = pl.program_id(0), pl.program_id(1)
    slot = step // parts
    count, width = own_ref.shape
    rows = width // HALVES
    steps = panels_ref.shape[0]

    def fetch(i):
        entry = ordered_slot(window_ref, last, i // parts) * parts + i % parts
        return pltpu.make_async_copy(panels_hbm.at[entry], panels_ref.at[i], panel_sem.at[i])

    @pl.when((step == 0) & (half == 0))
    def _():
        small = ((window_hbm, window_ref), (kept_hbm, kept_ref), (index_hbm, index_ref), (table_hbm, table_ref))
        copies = [pltpu.make_async_copy(src, dst, small_sem.at[i]) for i, (src, dst) in enumerate(small)]
        load_own = pltpu.make_async_copy(own_hbm, own_ref, own_sem)
        for copy in copies:
            copy.start()
        load_own.start()
        for copy in copies:
            copy.wait()
        for i in range(steps):
            @pl.when(kept_ref[0, i // parts] > 0)
            def _():
                fetch(i).start()
        load_own.wait()
        for h in range(HALVES):
            own_t[h, :ONES] = jnp.ones((ONES, count), jnp.bfloat16)
            own_t[h, ONES:] = own_ref[:, h * rows:(h + 1) * rows].T

    kept = kept_ref[0, slot] > 0

    @pl.when(kept & (half == 0))
    def _():
        fetch(step).wait()

    @pl.when(kept)
    def _():
        scale = table_ref[index_ref[0, slot]] / (count - 1)
        own_sum = jnp.dot(
            own_t[half, ONES:], jnp.ones((count, 128), jnp.bfloat16), preferred_element_type=jnp.float32
        )
        for first in range(0, out_ref.shape[1], 256):
            panel = panels_ref[step, :, first:first + 256]
            products = jnp.dot(own_t[half], panel, preferred_element_type=jnp.float32)
            panel_mean = products[:1] * (scale / count)
            for part in range(0, panel.shape[1], 128):
                here = slice(part, part + 128)
                value = scale * products[ONES:, here] - own_sum * panel_mean[:, here]
                out_ref[:, first + part:first + part + 128] = value.astype(jnp.bfloat16)

    @pl.when(jnp.logical_not(kept))
    def _():
        out_ref[...] = jnp.zeros_like(out_ref)


def tiles(own, panels, window_blocks, kept_tiles, taper_index, taper_table, last):
    count, width = own.shape
    steps, _, part = panels.shape
    parts = width // part
    dma = pltpu.SemaphoreType.DMA
    return pl.pallas_call(
        functools.partial(tile_kernel, parts, last),
        out_shape=jax.ShapeDtypeStruct((width, steps * part), jnp.bfloat16),
        grid=(steps, HALVES),
        in_specs=[pl.BlockSpec(memory_space=pl.ANY)] * 6,
        out_specs=pl.BlockSpec((width // HALVES, part), lambda i, h: (h, i)),
        scratch_shapes=[
            pltpu.SMEM(window_blocks.shape, jnp.int32),
            pltpu.SMEM(kept_tiles.shape, jnp.int32),
            pltpu.SMEM(taper_index.shape, jnp.int32),
            pltpu.SMEM(taper_table.shape, jnp.float32),
            pltpu.VMEM(own.shape, jnp.bfloat16),
            pltpu.VMEM(panels.shape, jnp.bfloat16),
            pltpu.VMEM((HALVES, ONES + width // HALVES, count), jnp.bfloat16),
            dma((4,)), dma, dma((steps,)),
        ],
        compiler_params=pltpu.CompilerParams(
            dimension_semantics=("arbitrary", "arbitrary"), vmem_limit_bytes=60 * 2**20
        ),
        name="tiles",
    )(window_blocks, kept_tiles, taper_index, taper_table, own, panels)


def per_device(row_count, col_count, mock_maps, window_blocks, kept_tiles, taper_index, taper_table):
    own, panels = gather(mock_maps, window_blocks, row_count, col_count)
    own = own.reshape(-1, own.shape[-1])
    panels = panels.reshape(panels.shape[0], -1, panels.shape[-1])
    last = row_count * col_count - 1
    return tiles(own, panels, window_blocks, kept_tiles, taper_index, taper_table, last)


def solution(mesh):
    in_specs = (P("col", "row"), P(), P(("row", "col"), None), P(("row", "col"), None), P())
    out_specs = P(("row", "col"), None)
    return jax.shard_map(
        functools.partial(per_device, mesh.shape["row"], mesh.shape["col"]),
        mesh=mesh, in_specs=in_specs, out_specs=out_specs, check_vma=False,
    )
```

```python
import functools

import jax
import jax.numpy as jnp
from jax import lax
from jax.experimental import pallas as pl
from jax.experimental.pallas import tpu as pltpu
from jax.sharding import PartitionSpec as P

MESH = pl.DeviceIdType.MESH
WINDOW = 4
CORES = 2
ALONG_Z = 4


def gather_kernel(
    row_count, col_count, window_ref, maps_ref, own_ref, panels_ref,
    maps, for_twin, mine, from_twin, summed, from_y, piece,
    twin_send, twin_recv, ysum_send, ysum_recv,
    z_send, x_send, y_send, core_send, panel_recv,
    own_send, own_recv, local_sem,
):
    ny, nx, nz = row_count // CORES, col_count // ALONG_Z, ALONG_Z
    row, col = lax.axis_index("row"), lax.axis_index("col")
    y, core = row // CORES, row % CORES
    z, x = col // nx, col % nx
    twin = y * CORES + (1 - core)
    width = own_ref.shape[2]
    part = panels_ref.shape[3]

    load_maps = pltpu.make_async_copy(maps_ref, maps, local_sem.at[2])
    load_maps.start()

    def row_of(d):
        return lax.rem(y + d, ny) * CORES + core

    barrier = pltpu.get_barrier_semaphore()
    peers = [(row, lax.rem(col + d, col_count)) for d in range(1, col_count)]
    peers += [(twin, col)] + [(row_of(d), col) for d in range(1, ny)]
    for peer in peers:
        pl.semaphore_signal(barrier, inc=1, device_id=peer, device_id_type=MESH)

    last = row_count * col_count - 1
    is_middle, rank, seen = [], [], 0
    for t in range(WINDOW):
        block = window_ref[t]
        is_middle.append(jnp.minimum(block, 1) * jnp.minimum(last - block, 1))
        rank.append(seen)
        seen = seen + is_middle[t]

    def masked(slot, offset):
        block = jnp.int32(0)
        for t in range(WINDOW):
            chosen = is_middle[t] * (1 - jnp.minimum(jnp.abs(rank[t] + 1 - slot), 1))
            block = block + chosen * window_ref[t]
        block = block + last * (1 - jnp.minimum(jnp.abs(slot - (WINDOW - 1)), 1))
        found = jnp.zeros((maps.shape[0], part), jnp.float32)
        for j in range(col_count):
            here = 1 - jnp.minimum(jnp.abs(block - (row * col_count + j)), 1)
            columns = maps[:, pl.ds(pl.multiple_of(j * width + offset, 128), part)]
            found = found + columns.astype(jnp.float32) * here.astype(jnp.float32)
        return found.astype(jnp.bfloat16)

    pl.semaphore_wait(barrier, len(peers))

    started = []

    def send(src, dst, send_sem, recv_sem, device):
        copy = pltpu.make_async_remote_copy(
            src_ref=src, dst_ref=dst, send_sem=send_sem, recv_sem=recv_sem,
            device_id=device, device_id_type=MESH,
        )
        copy.start()
        return copy

    def send_own(d):
        dest = lax.rem(col + d, col_count)
        columns = pl.ds(pl.multiple_of(dest * width, 128), width)
        started.append(send(
            maps_ref.at[:, columns], own_ref.at[col],
            own_send.at[d], own_recv.at[col], (row, dest),
        ))

    pending = sorted(range(1, col_count), key=lambda d: (d % nx != 0, abs(d - col_count // 2)))
    along_z = sum(d % nx == 0 for d in pending)

    def send_some(count):
        for _ in range(min(count, len(pending))):
            send_own(pending.pop(0))

    def slot(r, c):
        return panels_ref.at[r, c]

    def arrived(r, c):
        pltpu.make_async_remote_copy(
            src_ref=slot(r, c), dst_ref=slot(r, c), send_sem=core_send.at[r, c],
            recv_sem=panel_recv.at[r, c], device_id=(row, col), device_id_type=MESH,
        ).wait_recv()

    def out(src, r, c, send_sem, device, waiting):
        copy = pltpu.make_async_remote_copy(
            src_ref=src, dst_ref=slot(r, c), send_sem=send_sem,
            recv_sem=panel_recv.at[r, c], device_id=device, device_id_type=MESH,
        )
        if waiting:
            copy.wait_send()
        else:
            copy.start()

    def z_out(src, zz, up, waiting):
        to = z + 1 if up else z - 1

        @pl.when(to < nz if up else to >= 0)
        def _():
            c = zz * nx + x
            out(src, row, c, z_send.at[int(up), zz], (row, to * nx + x), waiting)

    def x_out(src, zz, waiting):
        c = zz * nx + x
        for d in range(1, nx):
            out(src, row, c, x_send.at[d, zz], (row, z * nx + lax.rem(x + d, nx)), waiting)

    def y_out(src, c, waiting):
        for d in range(1, ny):
            out(src, row, c, y_send.at[d, c], (row_of(d), col), waiting)

    def core_out(src, r, c, waiting):
        out(src, r, c, core_send.at[r, c], (twin, col), waiting)

    def at_z(d, body):
        if d == 0:
            body(z, None)
            return

        @pl.when(z >= d)
        def _():
            body(z - d, True)

        @pl.when(z + d < nz)
        def _():
            body(z + d, False)

    def own_event(src, waiting):
        z_out(src, z, True, waiting)
        z_out(src, z, False, waiting)
        y_out(src, col, waiting)
        x_out(src, z, waiting)
        core_out(src, row, col, waiting)

    def z_event(waiting, zz, up):
        c = zz * nx + x
        src = slot(row, c)
        if not waiting:
            arrived(row, c)
        z_out(src, zz, up, waiting)
        y_out(src, c, waiting)
        x_out(src, zz, waiting)
        core_out(src, row, c, waiting)

    def x_event(waiting, zz, up):
        for d in range(1, nx):
            c = zz * nx + lax.rem(x + d, nx)
            if not waiting:
                arrived(row, c)
            y_out(slot(row, c), c, waiting)
            core_out(slot(row, c), row, c, waiting)

    def y_event(waiting, own_x, zz, up):
        for dx in ([0] if own_x else range(1, nx)):
            c = zz * nx + lax.rem(x + dx, nx)
            for d in range(1, ny):
                r = row_of(d)
                if not waiting:
                    arrived(r, c)
                core_out(slot(r, c), r, c, waiting)

    def events(waiting):
        if waiting:
            own_event(piece, True)
        for d in range(1, nz):
            at_z(d, functools.partial(z_event, waiting))
            if d == nz - 2 and not waiting:
                send_some(along_z)
            at_z(d - 1, functools.partial(x_event, waiting))
        if not waiting:
            send_some(col_count)
        at_z(nz - 1, functools.partial(x_event, waiting))
        for d in range(nz):
            at_z(d, functools.partial(y_event, waiting, True))
            at_z(d, functools.partial(y_event, waiting, False))

    keep_own = pltpu.make_async_copy(
        maps_ref.at[:, pl.ds(pl.multiple_of(col * width, 128), width)], own_ref.at[col], local_sem.at[0]
    )
    keep_own.start()
    direct = part == width and row_count == WINDOW
    ends = lax.rem(row, row_count - 1) == 0

    def y_sum(d):
        return pltpu.make_async_remote_copy(
            src_ref=summed.at[d], dst_ref=from_y.at[ny - d], send_sem=ysum_send.at[d],
            recv_sem=ysum_recv.at[ny - d], device_id=(row_of(d), col), device_id_type=MESH,
        )

    if direct:
        first = pl.multiple_of((row // (row_count - 1)) * ((col_count - 1) * width), 128)
        held_piece = maps_ref.at[:, pl.ds(first, width)]

        @pl.when(ends)
        def _():
            own_event(held_piece, False)
            pltpu.make_async_copy(held_piece, slot(row, col), local_sem.at[1]).start()

        load_maps.wait()
        for_twin[0] = masked(1 + core, 0)
        mine[0] = masked(2 - core, 0)
        twin_copy = send(for_twin, from_twin, twin_send, twin_recv, (twin, col))
        twin_copy.wait_recv()
        summed[1] = mine[0] + from_twin[0]

        @pl.when(ends)
        def _():
            y_sum(1).start()

        @pl.when(jnp.logical_not(ends))
        def _():
            y_sum(1).wait_recv()
            piece[...] = summed[1] + from_y[1]
            own_event(piece, False)
            pltpu.make_async_copy(piece, slot(row, col), local_sem.at[1]).start()
    else:
        load_maps.wait()
        for d in range(ny):
            for k, held in ((1 - core, for_twin), (core, mine)):
                first = (lax.rem(y + d, ny) * CORES + k) * part
                held[d] = masked(first // width, lax.rem(first, width))
        twin_copy = send(for_twin, from_twin, twin_send, twin_recv, (twin, col))
        twin_copy.wait_recv()
        for d in range(ny):
            summed[d] = mine[d] + from_twin[d]
        for d in range(1, ny):
            y_sum(d).start()
        total = summed[0]
        for d in range(1, ny):
            y_sum(d).wait_recv()
            total = total + from_y[ny - d]
        piece[...] = total
        own_event(piece, False)
        pltpu.make_async_copy(piece, slot(row, col), local_sem.at[1]).start()
    events(False)

    for d in range(ny):
        r = lax.rem(y + d, ny) * CORES + (1 - core)

        @pl.loop(0, col_count)
        def _(c):
            arrived(r, c)

    for d in range(1, col_count):
        source = lax.rem(col + d, col_count)
        pltpu.make_async_remote_copy(
            src_ref=own_ref.at[source], dst_ref=own_ref.at[source], send_sem=own_send.at[d],
            recv_sem=own_recv.at[source], device_id=(row, source), device_id_type=MESH,
        ).wait_recv()
    twin_copy.wait_send()
    for copy in started:
        copy.wait_send()
    if direct:
        @pl.when(ends)
        def _():
            y_sum(1).wait_send()
    else:
        for d in range(1, ny):
            y_sum(d).wait_send()
    events(True)
    keep_own.wait()
    pltpu.make_async_copy(piece, slot(row, col), local_sem.at[1]).wait()


def gather(mock_maps, window_blocks, row_count, col_count):
    mocks = mock_maps.shape[0]
    width = mock_maps.shape[1] // col_count
    part = WINDOW * width // row_count
    ny = row_count // CORES
    nx = col_count // ALONG_Z
    dma = pltpu.SemaphoreType.DMA
    shares = 1 if part == width else ny
    return pl.pallas_call(
        functools.partial(gather_kernel, row_count, col_count),
        out_shape=(
            jax.ShapeDtypeStruct((col_count, mocks, width), jnp.bfloat16),
            jax.ShapeDtypeStruct((row_count, col_count, mocks, part), jnp.bfloat16),
        ),
        in_specs=[pl.BlockSpec(memory_space=pltpu.SMEM), pl.BlockSpec(memory_space=pl.ANY)],
        out_specs=(pl.BlockSpec(memory_space=pl.ANY), pl.BlockSpec(memory_space=pl.ANY)),
        scratch_shapes=[
            pltpu.VMEM(mock_maps.shape, jnp.bfloat16),
            pltpu.VMEM((shares, mocks, part), jnp.bfloat16),
            pltpu.VMEM((shares, mocks, part), jnp.bfloat16),
            pltpu.VMEM((shares, mocks, part), jnp.bfloat16),
            pltpu.VMEM((ny, mocks, part), jnp.bfloat16),
            pltpu.VMEM((ny, mocks, part), jnp.bfloat16),
            pltpu.VMEM((mocks, part), jnp.bfloat16),
            dma, dma, dma((ny,)), dma((ny,)),
            dma((2, ALONG_Z)), dma((nx, ALONG_Z)), dma((ny, col_count)),
            dma((row_count, col_count)), dma((row_count, col_count)),
            dma((col_count,)), dma((col_count,)), dma((3,)),
        ],
        compiler_params=pltpu.CompilerParams(
            collective_id=0, has_side_effects=True, vmem_limit_bytes=60 * 2**20
        ),
        name="gather",
    )(window_blocks, mock_maps)


def ordered_slot(window_ref, last, slot):
    block = window_ref[slot]
    rank = jnp.int32(1)
    for t in range(WINDOW):
        middle = (t < slot) & (window_ref[t] != 0) & (window_ref[t] != last)
        rank = rank + middle.astype(jnp.int32)
    return jnp.where(block == 0, 0, jnp.where(block == last, WINDOW - 1, rank))


ONES = 16
HALVES = 2


def tile_kernel(
    parts, last, window_hbm, kept_hbm, index_hbm, table_hbm, own_hbm, panels_hbm, out_ref,
    window_ref, kept_ref, index_ref, table_ref, own_ref, panels_ref, own_t, own_sum, small_sem, own_sem, panel_sem,
):
    step, half = pl.program_id(0), pl.program_id(1)
    slot = step // parts
    count, width = own_ref.shape
    rows = width // HALVES
    steps = panels_ref.shape[0]

    def fetch(i):
        entry = ordered_slot(window_ref, last, i // parts) * parts + i % parts
        return pltpu.make_async_copy(panels_hbm.at[entry], panels_ref.at[i], panel_sem.at[i])

    @pl.when((step == 0) & (half == 0))
    def _():
        small = ((window_hbm, window_ref), (kept_hbm, kept_ref), (index_hbm, index_ref), (table_hbm, table_ref))
        copies = [pltpu.make_async_copy(src, dst, small_sem.at[i]) for i, (src, dst) in enumerate(small)]
        load_own = pltpu.make_async_copy(own_hbm, own_ref, own_sem)
        for copy in copies:
            copy.start()
        load_own.start()
        for copy in copies:
            copy.wait()
        for i in range(steps):
            @pl.when(kept_ref[0, i // parts] > 0)
            def _():
                fetch(i).start()
        load_own.wait()
        for h in range(HALVES):
            own_t[h, :ONES] = jnp.ones((ONES, count), jnp.bfloat16)
            own_t[h, ONES:] = own_ref[:, h * rows:(h + 1) * rows].T
            own_sum[h] = jnp.dot(
                own_t[h, ONES:], jnp.ones((count, 128), jnp.bfloat16), preferred_element_type=jnp.float32
            )

    kept = kept_ref[0, slot] > 0

    @pl.when(kept & (half == 0))
    def _():
        fetch(step).wait()

    @pl.when(kept)
    def _():
        scale = table_ref[index_ref[0, slot]] / (count - 1)
        panel = panels_ref[step]
        panel_mean = None
        for first in range(0, rows, rows // 2):
            skip = ONES if panel_mean is None else 0
            left = own_t[half, pl.ds(first + ONES - skip, rows // 2 + skip)]
            products = jnp.dot(left, panel, preferred_element_type=jnp.float32)
            if panel_mean is None:
                panel_mean = products[:1] * (scale / count)
            sums = own_sum[half, pl.ds(first, rows // 2)]
            for part in range(0, panel.shape[1], 128):
                here = slice(part, part + 128)
                value = scale * products[skip:, here] - sums * panel_mean[:, here]
                out_ref[first:first + rows // 2, here] = value.astype(jnp.bfloat16)

    @pl.when(jnp.logical_not(kept))
    def _():
        out_ref[...] = jnp.zeros_like(out_ref)


def tiles(own, panels, window_blocks, kept_tiles, taper_index, taper_table, last):
    count, width = own.shape
    steps, _, part = panels.shape
    parts = width // part
    dma = pltpu.SemaphoreType.DMA
    return pl.pallas_call(
        functools.partial(tile_kernel, parts, last),
        out_shape=jax.ShapeDtypeStruct((width, steps * part), jnp.bfloat16),
        grid=(steps, HALVES),
        in_specs=[pl.BlockSpec(memory_space=pl.ANY)] * 6,
        out_specs=pl.BlockSpec((width // HALVES, part), lambda i, h: (h, i)),
        scratch_shapes=[
            pltpu.SMEM(window_blocks.shape, jnp.int32),
            pltpu.SMEM(kept_tiles.shape, jnp.int32),
            pltpu.SMEM(taper_index.shape, jnp.int32),
            pltpu.SMEM(taper_table.shape, jnp.float32),
            pltpu.VMEM(own.shape, jnp.bfloat16),
            pltpu.VMEM(panels.shape, jnp.bfloat16),
            pltpu.VMEM((HALVES, ONES + width // HALVES, count), jnp.bfloat16),
            pltpu.VMEM((HALVES, width // HALVES, 128), jnp.float32),
            dma((4,)), dma, dma((steps,)),
        ],
        compiler_params=pltpu.CompilerParams(
            dimension_semantics=("arbitrary", "arbitrary"), vmem_limit_bytes=60 * 2**20
        ),
        name="tiles",
    )(window_blocks, kept_tiles, taper_index, taper_table, own, panels)


def per_device(row_count, col_count, mock_maps, window_blocks, kept_tiles, taper_index, taper_table):
    own, panels = gather(mock_maps, window_blocks, row_count, col_count)
    own = own.reshape(-1, own.shape[-1])
    panels = panels.reshape(panels.shape[0], -1, panels.shape[-1])
    last = row_count * col_count - 1
    return tiles(own, panels, window_blocks, kept_tiles, taper_index, taper_table, last)


def solution(mesh):
    in_specs = (P("col", "row"), P(), P(("row", "col"), None), P(("row", "col"), None), P())
    out_specs = P(("row", "col"), None)
    return jax.shard_map(
        functools.partial(per_device, mesh.shape["row"], mesh.shape["col"]),
        mesh=mesh, in_specs=in_specs, out_specs=out_specs, check_vma=False,
    )
```

```python
import functools

import jax
import jax.numpy as jnp
from jax import lax
from jax.experimental import pallas as pl
from jax.experimental.pallas import tpu as pltpu
from jax.sharding import PartitionSpec as P

MESH = pl.DeviceIdType.MESH
WINDOW = 4
CORES = 2
ALONG_Z = 4


def gather_kernel(
    row_count, col_count, window_ref, maps_ref, own_ref, panels_ref,
    maps, for_twin, mine, from_twin, summed, from_y, piece,
    twin_send, twin_recv, ysum_send, ysum_recv,
    z_send, x_send, y_send, core_send, panel_recv,
    own_send, own_recv, local_sem,
):
    ny, nx, nz = row_count // CORES, col_count // ALONG_Z, ALONG_Z
    row, col = lax.axis_index("row"), lax.axis_index("col")
    y, core = row // CORES, row % CORES
    z, x = col // nx, col % nx
    twin = y * CORES + (1 - core)
    width = own_ref.shape[2]
    part = panels_ref.shape[3]

    load_maps = pltpu.make_async_copy(maps_ref, maps, local_sem.at[2])
    load_maps.start()

    def row_of(d):
        return lax.rem(y + d, ny) * CORES + core

    barrier = pltpu.get_barrier_semaphore()
    peers = [(row, lax.rem(col + d, col_count)) for d in range(1, col_count)]
    peers += [(twin, col)] + [(row_of(d), col) for d in range(1, ny)]
    for peer in peers:
        pl.semaphore_signal(barrier, inc=1, device_id=peer, device_id_type=MESH)

    last = row_count * col_count - 1
    is_middle, rank, seen = [], [], 0
    for t in range(WINDOW):
        block = window_ref[t]
        is_middle.append(jnp.minimum(block, 1) * jnp.minimum(last - block, 1))
        rank.append(seen)
        seen = seen + is_middle[t]

    def masked(slot, offset):
        block = jnp.int32(0)
        for t in range(WINDOW):
            chosen = is_middle[t] * (1 - jnp.minimum(jnp.abs(rank[t] + 1 - slot), 1))
            block = block + chosen * window_ref[t]
        block = block + last * (1 - jnp.minimum(jnp.abs(slot - (WINDOW - 1)), 1))
        found = jnp.zeros((maps.shape[0], part), jnp.float32)
        for j in range(col_count):
            here = 1 - jnp.minimum(jnp.abs(block - (row * col_count + j)), 1)
            columns = maps[:, pl.ds(pl.multiple_of(j * width + offset, 128), part)]
            found = found + columns.astype(jnp.float32) * here.astype(jnp.float32)
        return found.astype(jnp.bfloat16)

    pl.semaphore_wait(barrier, len(peers))

    started = []

    def send(src, dst, send_sem, recv_sem, device):
        copy = pltpu.make_async_remote_copy(
            src_ref=src, dst_ref=dst, send_sem=send_sem, recv_sem=recv_sem,
            device_id=device, device_id_type=MESH,
        )
        copy.start()
        return copy

    def send_own(d):
        dest = lax.rem(col + d, col_count)
        columns = pl.ds(pl.multiple_of(dest * width, 128), width)
        started.append(send(
            maps_ref.at[:, columns], own_ref.at[col],
            own_send.at[d], own_recv.at[col], (row, dest),
        ))

    pending = sorted(
        range(1, col_count),
        key=lambda d: (1, abs(d - col_count // 2)) if d % nx else (0, -abs(d - col_count // 2)),
    )
    along_z = sum(d % nx == 0 for d in pending)

    def send_some(count):
        for _ in range(min(count, len(pending))):
            send_own(pending.pop(0))

    def slot(r, c):
        return panels_ref.at[r, c]

    def arrived(r, c):
        pltpu.make_async_remote_copy(
            src_ref=slot(r, c), dst_ref=slot(r, c), send_sem=core_send.at[r, c],
            recv_sem=panel_recv.at[r, c], device_id=(row, col), device_id_type=MESH,
        ).wait_recv()

    def out(src, r, c, send_sem, device, waiting):
        copy = pltpu.make_async_remote_copy(
            src_ref=src, dst_ref=slot(r, c), send_sem=send_sem,
            recv_sem=panel_recv.at[r, c], device_id=device, device_id_type=MESH,
        )
        if waiting:
            copy.wait_send()
        else:
            copy.start()

    def z_out(src, zz, up, waiting):
        to = z + 1 if up else z - 1

        @pl.when(to < nz if up else to >= 0)
        def _():
            c = zz * nx + x
            out(src, row, c, z_send.at[int(up), zz], (row, to * nx + x), waiting)

    def x_out(src, zz, waiting):
        c = zz * nx + x
        for d in range(1, nx):
            out(src, row, c, x_send.at[d, zz], (row, z * nx + lax.rem(x + d, nx)), waiting)

    def y_out(src, c, waiting):
        for d in range(1, ny):
            out(src, row, c, y_send.at[d, c], (row_of(d), col), waiting)

    def core_out(src, r, c, waiting):
        out(src, r, c, core_send.at[r, c], (twin, col), waiting)

    def at_z(d, body):
        if d == 0:
            body(z, None)
            return

        @pl.when(z >= d)
        def _():
            body(z - d, True)

        @pl.when(z + d < nz)
        def _():
            body(z + d, False)

    def own_event(src, waiting):
        z_out(src, z, True, waiting)
        z_out(src, z, False, waiting)
        y_out(src, col, waiting)
        x_out(src, z, waiting)
        core_out(src, row, col, waiting)

    def z_event(waiting, zz, up):
        c = zz * nx + x
        src = slot(row, c)
        if not waiting:
            arrived(row, c)
        z_out(src, zz, up, waiting)
        y_out(src, c, waiting)
        x_out(src, zz, waiting)
        core_out(src, row, c, waiting)

    def x_event(waiting, zz, up):
        for d in range(1, nx):
            c = zz * nx + lax.rem(x + d, nx)
            if not waiting:
                arrived(row, c)
            y_out(slot(row, c), c, waiting)
            core_out(slot(row, c), row, c, waiting)

    def y_event(waiting, own_x, zz, up):
        for dx in ([0] if own_x else range(1, nx)):
            c = zz * nx + lax.rem(x + dx, nx)
            for d in range(1, ny):
                r = row_of(d)
                if not waiting:
                    arrived(r, c)
                core_out(slot(r, c), r, c, waiting)

    def events(waiting):
        if waiting:
            own_event(piece, True)
        for d in range(1, nz):
            at_z(d, functools.partial(z_event, waiting))
            if d == nz - 2 and not waiting:
                send_some(along_z - (2 if direct else 1))
            at_z(d - 1, functools.partial(x_event, waiting))
        if not waiting:
            send_some(col_count)
        at_z(nz - 1, functools.partial(x_event, waiting))
        for d in range(nz):
            at_z(d, functools.partial(y_event, waiting, True))
            at_z(d, functools.partial(y_event, waiting, False))

    keep_own = pltpu.make_async_copy(
        maps_ref.at[:, pl.ds(pl.multiple_of(col * width, 128), width)], own_ref.at[col], local_sem.at[0]
    )
    keep_own.start()
    direct = part == width and row_count == WINDOW
    ends = lax.rem(row, row_count - 1) == 0

    def y_sum(d):
        return pltpu.make_async_remote_copy(
            src_ref=summed.at[d], dst_ref=from_y.at[ny - d], send_sem=ysum_send.at[d],
            recv_sem=ysum_recv.at[ny - d], device_id=(row_of(d), col), device_id_type=MESH,
        )

    if direct:
        first = pl.multiple_of((row // (row_count - 1)) * ((col_count - 1) * width), 128)
        held_piece = maps_ref.at[:, pl.ds(first, width)]

        @pl.when(ends)
        def _():
            own_event(held_piece, False)
            pltpu.make_async_copy(held_piece, slot(row, col), local_sem.at[1]).start()

        send_some(1)
        load_maps.wait()
        for_twin[0] = masked(1 + core, 0)
        mine[0] = masked(2 - core, 0)
        twin_copy = send(for_twin, from_twin, twin_send, twin_recv, (twin, col))
        twin_copy.wait_recv()
        summed[1] = mine[0] + from_twin[0]

        @pl.when(ends)
        def _():
            y_sum(1).start()

        @pl.when(jnp.logical_not(ends))
        def _():
            y_sum(1).wait_recv()
            piece[...] = summed[1] + from_y[1]
            own_event(piece, False)
            pltpu.make_async_copy(piece, slot(row, col), local_sem.at[1]).start()
    else:
        load_maps.wait()
        for d in range(ny):
            for k, held in ((1 - core, for_twin), (core, mine)):
                first = (lax.rem(y + d, ny) * CORES + k) * part
                held[d] = masked(first // width, lax.rem(first, width))
        twin_copy = send(for_twin, from_twin, twin_send, twin_recv, (twin, col))
        twin_copy.wait_recv()
        for d in range(ny):
            summed[d] = mine[d] + from_twin[d]
        for d in range(1, ny):
            y_sum(d).start()
        total = summed[0]
        for d in range(1, ny):
            y_sum(d).wait_recv()
            total = total + from_y[ny - d]
        piece[...] = total
        own_event(piece, False)
        pltpu.make_async_copy(piece, slot(row, col), local_sem.at[1]).start()
    send_some(1)
    events(False)

    for d in range(ny):
        r = lax.rem(y + d, ny) * CORES + (1 - core)

        @pl.loop(0, col_count)
        def _(c):
            arrived(r, c)

    for d in range(1, col_count):
        source = lax.rem(col + d, col_count)
        pltpu.make_async_remote_copy(
            src_ref=own_ref.at[source], dst_ref=own_ref.at[source], send_sem=own_send.at[d],
            recv_sem=own_recv.at[source], device_id=(row, source), device_id_type=MESH,
        ).wait_recv()
    twin_copy.wait_send()
    for copy in started:
        copy.wait_send()
    if direct:
        @pl.when(ends)
        def _():
            y_sum(1).wait_send()
    else:
        for d in range(1, ny):
            y_sum(d).wait_send()
    events(True)
    keep_own.wait()
    pltpu.make_async_copy(piece, slot(row, col), local_sem.at[1]).wait()


def gather(mock_maps, window_blocks, row_count, col_count):
    mocks = mock_maps.shape[0]
    width = mock_maps.shape[1] // col_count
    part = WINDOW * width // row_count
    ny = row_count // CORES
    nx = col_count // ALONG_Z
    dma = pltpu.SemaphoreType.DMA
    shares = 1 if part == width else ny
    return pl.pallas_call(
        functools.partial(gather_kernel, row_count, col_count),
        out_shape=(
            jax.ShapeDtypeStruct((col_count, mocks, width), jnp.bfloat16),
            jax.ShapeDtypeStruct((row_count, col_count, mocks, part), jnp.bfloat16),
        ),
        in_specs=[pl.BlockSpec(memory_space=pltpu.SMEM), pl.BlockSpec(memory_space=pl.ANY)],
        out_specs=(pl.BlockSpec(memory_space=pl.ANY), pl.BlockSpec(memory_space=pl.ANY)),
        scratch_shapes=[
            pltpu.VMEM(mock_maps.shape, jnp.bfloat16),
            pltpu.VMEM((shares, mocks, part), jnp.bfloat16),
            pltpu.VMEM((shares, mocks, part), jnp.bfloat16),
            pltpu.VMEM((shares, mocks, part), jnp.bfloat16),
            pltpu.VMEM((ny, mocks, part), jnp.bfloat16),
            pltpu.VMEM((ny, mocks, part), jnp.bfloat16),
            pltpu.VMEM((mocks, part), jnp.bfloat16),
            dma, dma, dma((ny,)), dma((ny,)),
            dma((2, ALONG_Z)), dma((nx, ALONG_Z)), dma((ny, col_count)),
            dma((row_count, col_count)), dma((row_count, col_count)),
            dma((col_count,)), dma((col_count,)), dma((3,)),
        ],
        compiler_params=pltpu.CompilerParams(
            collective_id=0, has_side_effects=True, vmem_limit_bytes=60 * 2**20
        ),
        name="gather",
    )(window_blocks, mock_maps)


def ordered_slot(window_ref, last, slot):
    block = window_ref[slot]
    rank = jnp.int32(1)
    for t in range(WINDOW):
        middle = (t < slot) & (window_ref[t] != 0) & (window_ref[t] != last)
        rank = rank + middle.astype(jnp.int32)
    return jnp.where(block == 0, 0, jnp.where(block == last, WINDOW - 1, rank))


ONES = 16
HALVES = 2


def tile_kernel(
    parts, last, window_hbm, kept_hbm, index_hbm, table_hbm, own_hbm, panels_hbm, out_ref,
    window_ref, kept_ref, index_ref, table_ref, own_ref, panels_ref, own_t, own_sum, small_sem, own_sem, panel_sem,
):
    step, half = pl.program_id(0), pl.program_id(1)
    slot = step // parts
    count, width = own_ref.shape
    rows = width // HALVES
    steps = panels_ref.shape[0]

    def fetch(i):
        entry = ordered_slot(window_ref, last, i // parts) * parts + i % parts
        return pltpu.make_async_copy(panels_hbm.at[entry], panels_ref.at[i], panel_sem.at[i])

    @pl.when((step == 0) & (half == 0))
    def _():
        small = ((window_hbm, window_ref), (kept_hbm, kept_ref), (index_hbm, index_ref), (table_hbm, table_ref))
        copies = [pltpu.make_async_copy(src, dst, small_sem.at[i]) for i, (src, dst) in enumerate(small)]
        load_own = pltpu.make_async_copy(own_hbm, own_ref, own_sem)
        for copy in copies:
            copy.start()
        load_own.start()
        for copy in copies:
            copy.wait()
        for i in range(steps):
            @pl.when(kept_ref[0, i // parts] > 0)
            def _():
                fetch(i).start()
        load_own.wait()
        for h in range(HALVES):
            own_t[h, :ONES] = jnp.ones((ONES, count), jnp.bfloat16)
            own_t[h, ONES:] = own_ref[:, h * rows:(h + 1) * rows].T
            own_sum[h] = jnp.dot(
                own_t[h, ONES:], jnp.ones((count, 128), jnp.bfloat16), preferred_element_type=jnp.float32
            )

    kept = kept_ref[0, slot] > 0

    @pl.when(kept & (half == 0))
    def _():
        fetch(step).wait()

    @pl.when(kept)
    def _():
        scale = table_ref[index_ref[0, slot]] / (count - 1)
        panel = panels_ref[step]
        panel_mean = None
        for first in range(0, rows, rows // 2):
            skip = ONES if panel_mean is None else 0
            left = own_t[half, pl.ds(first + ONES - skip, rows // 2 + skip)]
            products = jnp.dot(left, panel, preferred_element_type=jnp.float32)
            if panel_mean is None:
                panel_mean = products[:1] * (scale / count)
            sums = own_sum[half, pl.ds(first, rows // 2)]
            for part in range(0, panel.shape[1], 128):
                here = slice(part, part + 128)
                value = scale * products[skip:, here] - sums * panel_mean[:, here]
                out_ref[first:first + rows // 2, here] = value.astype(jnp.bfloat16)

    @pl.when(jnp.logical_not(kept))
    def _():
        out_ref[...] = jnp.zeros_like(out_ref)


def tiles(own, panels, window_blocks, kept_tiles, taper_index, taper_table, last):
    count, width = own.shape
    steps, _, part = panels.shape
    parts = width // part
    dma = pltpu.SemaphoreType.DMA
    return pl.pallas_call(
        functools.partial(tile_kernel, parts, last),
        out_shape=jax.ShapeDtypeStruct((width, steps * part), jnp.bfloat16),
        grid=(steps, HALVES),
        in_specs=[pl.BlockSpec(memory_space=pl.ANY)] * 6,
        out_specs=pl.BlockSpec((width // HALVES, part), lambda i, h: (h, i)),
        scratch_shapes=[
            pltpu.SMEM(window_blocks.shape, jnp.int32),
            pltpu.SMEM(kept_tiles.shape, jnp.int32),
            pltpu.SMEM(taper_index.shape, jnp.int32),
            pltpu.SMEM(taper_table.shape, jnp.float32),
            pltpu.VMEM(own.shape, jnp.bfloat16),
            pltpu.VMEM(panels.shape, jnp.bfloat16),
            pltpu.VMEM((HALVES, ONES + width // HALVES, count), jnp.bfloat16),
            pltpu.VMEM((HALVES, width // HALVES, 128), jnp.float32),
            dma((4,)), dma, dma((steps,)),
        ],
        compiler_params=pltpu.CompilerParams(
            dimension_semantics=("arbitrary", "arbitrary"), vmem_limit_bytes=60 * 2**20
        ),
        name="tiles",
    )(window_blocks, kept_tiles, taper_index, taper_table, own, panels)


def per_device(row_count, col_count, mock_maps, window_blocks, kept_tiles, taper_index, taper_table):
    own, panels = gather(mock_maps, window_blocks, row_count, col_count)
    own = own.reshape(-1, own.shape[-1])
    panels = panels.reshape(panels.shape[0], -1, panels.shape[-1])
    last = row_count * col_count - 1
    return tiles(own, panels, window_blocks, kept_tiles, taper_index, taper_table, last)


def solution(mesh):
    in_specs = (P("col", "row"), P(), P(("row", "col"), None), P(("row", "col"), None), P())
    out_specs = P(("row", "col"), None)
    return jax.shard_map(
        functools.partial(per_device, mesh.shape["row"], mesh.shape["col"]),
        mesh=mesh, in_specs=in_specs, out_specs=out_specs, check_vma=False,
    )
```

```python
import functools

import jax
import jax.numpy as jnp
from jax import lax
from jax.experimental import pallas as pl
from jax.experimental.pallas import tpu as pltpu
from jax.sharding import PartitionSpec as P

MESH = pl.DeviceIdType.MESH
WINDOW = 4
CORES = 2
ALONG_Z = 4


def gather_kernel(
    row_count, col_count, window_ref, maps_ref, own_ref, panels_ref,
    maps, for_twin, mine, from_twin, summed, from_y, piece,
    twin_send, twin_recv, ysum_send, ysum_recv,
    z_send, x_send, y_send, core_send, panel_recv,
    own_send, own_recv, local_sem,
):
    ny, nx, nz = row_count // CORES, col_count // ALONG_Z, ALONG_Z
    row, col = lax.axis_index("row"), lax.axis_index("col")
    y, core = row // CORES, row % CORES
    z, x = col // nx, col % nx
    twin = y * CORES + (1 - core)
    width = own_ref.shape[2]
    part = panels_ref.shape[3]

    load_maps = pltpu.make_async_copy(maps_ref, maps, local_sem.at[2])
    load_maps.start()

    def row_of(d):
        return lax.rem(y + d, ny) * CORES + core

    barrier = pltpu.get_barrier_semaphore()
    peers = [(row, lax.rem(col + d, col_count)) for d in range(1, col_count)]
    peers += [(twin, col)] + [(row_of(d), col) for d in range(1, ny)]
    for peer in peers:
        pl.semaphore_signal(barrier, inc=1, device_id=peer, device_id_type=MESH)

    last = row_count * col_count - 1
    is_middle, rank, seen = [], [], 0
    for t in range(WINDOW):
        block = window_ref[t]
        is_middle.append(jnp.minimum(block, 1) * jnp.minimum(last - block, 1))
        rank.append(seen)
        seen = seen + is_middle[t]

    def masked(slot, offset):
        block = jnp.int32(0)
        for t in range(WINDOW):
            chosen = is_middle[t] * (1 - jnp.minimum(jnp.abs(rank[t] + 1 - slot), 1))
            block = block + chosen * window_ref[t]
        block = block + last * (1 - jnp.minimum(jnp.abs(slot - (WINDOW - 1)), 1))
        found = jnp.zeros((maps.shape[0], part), jnp.float32)
        for j in range(col_count):
            here = 1 - jnp.minimum(jnp.abs(block - (row * col_count + j)), 1)
            columns = maps[:, pl.ds(pl.multiple_of(j * width + offset, 128), part)]
            found = found + columns.astype(jnp.float32) * here.astype(jnp.float32)
        return found.astype(jnp.bfloat16)

    direct = part == width and row_count == WINDOW
    load_maps.wait()
    if direct:
        for_twin[0] = masked(1 + core, 0)
        mine[0] = masked(2 - core, 0)

    pl.semaphore_wait(barrier, len(peers))

    started = []

    def send(src, dst, send_sem, recv_sem, device):
        copy = pltpu.make_async_remote_copy(
            src_ref=src, dst_ref=dst, send_sem=send_sem, recv_sem=recv_sem,
            device_id=device, device_id_type=MESH,
        )
        copy.start()
        return copy

    def send_own(d):
        dest = lax.rem(col + d, col_count)
        columns = pl.ds(pl.multiple_of(dest * width, 128), width)
        started.append(send(
            maps_ref.at[:, columns], own_ref.at[col],
            own_send.at[d], own_recv.at[col], (row, dest),
        ))

    pending = sorted(
        range(1, col_count),
        key=lambda d: (1, abs(d - col_count // 2)) if d % nx else (0, -abs(d - col_count // 2)),
    )
    along_z = sum(d % nx == 0 for d in pending)

    def send_some(count):
        for _ in range(min(count, len(pending))):
            send_own(pending.pop(0))

    def slot(r, c):
        return panels_ref.at[r, c]

    def arrived(r, c):
        pltpu.make_async_remote_copy(
            src_ref=slot(r, c), dst_ref=slot(r, c), send_sem=core_send.at[r, c],
            recv_sem=panel_recv.at[r, c], device_id=(row, col), device_id_type=MESH,
        ).wait_recv()

    def out(src, r, c, send_sem, device, waiting):
        copy = pltpu.make_async_remote_copy(
            src_ref=src, dst_ref=slot(r, c), send_sem=send_sem,
            recv_sem=panel_recv.at[r, c], device_id=device, device_id_type=MESH,
        )
        if waiting:
            copy.wait_send()
        else:
            copy.start()

    def z_out(src, zz, up, waiting):
        to = z + 1 if up else z - 1

        @pl.when(to < nz if up else to >= 0)
        def _():
            c = zz * nx + x
            out(src, row, c, z_send.at[int(up), zz], (row, to * nx + x), waiting)

    def x_out(src, zz, waiting):
        c = zz * nx + x
        for d in range(1, nx):
            out(src, row, c, x_send.at[d, zz], (row, z * nx + lax.rem(x + d, nx)), waiting)

    def y_out(src, c, waiting):
        for d in range(1, ny):
            out(src, row, c, y_send.at[d, c], (row_of(d), col), waiting)

    def core_out(src, r, c, waiting):
        out(src, r, c, core_send.at[r, c], (twin, col), waiting)

    def at_z(d, body):
        if d == 0:
            body(z, None)
            return

        @pl.when(z >= d)
        def _():
            body(z - d, True)

        @pl.when(z + d < nz)
        def _():
            body(z + d, False)

    def own_event(src, waiting, along_y=True):
        z_out(src, z, True, waiting)
        z_out(src, z, False, waiting)
        if along_y:
            y_out(src, col, waiting)
        x_out(src, z, waiting)
        core_out(src, row, col, waiting)

    def z_event(waiting, zz, up):
        c = zz * nx + x
        src = slot(row, c)
        if not waiting:
            arrived(row, c)
        z_out(src, zz, up, waiting)
        y_out(src, c, waiting)
        x_out(src, zz, waiting)
        core_out(src, row, c, waiting)

    def x_event(waiting, zz, up):
        for d in range(1, nx):
            c = zz * nx + lax.rem(x + d, nx)
            if not waiting:
                arrived(row, c)
            y_out(slot(row, c), c, waiting)
            core_out(slot(row, c), row, c, waiting)

    def y_event(waiting, own_x, zz, up):
        for dx in ([0] if own_x else range(1, nx)):
            c = zz * nx + lax.rem(x + dx, nx)
            for d in range(1, ny):
                r = row_of(d)
                if not waiting:
                    arrived(r, c)
                core_out(slot(r, c), r, c, waiting)

    def events(waiting):
        if waiting:
            own_event(piece, True)
        for d in range(1, nz):
            at_z(d, functools.partial(z_event, waiting))
            if d == nz - 2 and not waiting:
                send_some(along_z - (2 if direct else 1))
            at_z(d - 1, functools.partial(x_event, waiting))
            if d >= nz - 2 and not waiting:
                send_some(len(pending) // 2 if d == nz - 2 else col_count)
        at_z(nz - 1, functools.partial(x_event, waiting))
        for d in range(nz):
            at_z(d, functools.partial(y_event, waiting, True))
            at_z(d, functools.partial(y_event, waiting, False))

    keep_own = pltpu.make_async_copy(
        maps_ref.at[:, pl.ds(pl.multiple_of(col * width, 128), width)], own_ref.at[col], local_sem.at[0]
    )
    keep_own.start()
    ends = lax.rem(row, row_count - 1) == 0

    def y_sum(d):
        return pltpu.make_async_remote_copy(
            src_ref=summed.at[d], dst_ref=from_y.at[ny - d], send_sem=ysum_send.at[d],
            recv_sem=ysum_recv.at[ny - d], device_id=(row_of(d), col), device_id_type=MESH,
        )

    if direct:
        first = pl.multiple_of((row // (row_count - 1)) * ((col_count - 1) * width), 128)
        held_piece = maps_ref.at[:, pl.ds(first, width)]

        twin_copy = send(for_twin, from_twin, twin_send, twin_recv, (twin, col))

        @pl.when(ends)
        def _():
            own_event(held_piece, False, along_y=False)
            pltpu.make_async_copy(held_piece, slot(row, col), local_sem.at[1]).start()

        twin_copy.wait_recv()
        summed[1] = mine[0] + from_twin[0]

        @pl.when(ends)
        def _():
            y_sum(1).start()
            y_out(held_piece, col, False)

        send_some(1)

        @pl.when(jnp.logical_not(ends))
        def _():
            y_sum(1).wait_recv()
            piece[...] = summed[1] + from_y[1]
            own_event(piece, False)
            pltpu.make_async_copy(piece, slot(row, col), local_sem.at[1]).start()
    else:
        for d in range(ny):
            for k, held in ((1 - core, for_twin), (core, mine)):
                first = (lax.rem(y + d, ny) * CORES + k) * part
                held[d] = masked(first // width, lax.rem(first, width))
        twin_copy = send(for_twin, from_twin, twin_send, twin_recv, (twin, col))
        twin_copy.wait_recv()
        for d in range(ny):
            summed[d] = mine[d] + from_twin[d]
        for d in range(1, ny):
            y_sum(d).start()
        total = summed[0]
        for d in range(1, ny):
            y_sum(d).wait_recv()
            total = total + from_y[ny - d]
        piece[...] = total
        own_event(piece, False)
        pltpu.make_async_copy(piece, slot(row, col), local_sem.at[1]).start()
    send_some(1)
    events(False)

    for d in range(ny):
        r = lax.rem(y + d, ny) * CORES + (1 - core)

        @pl.loop(0, col_count)
        def _(c):
            arrived(r, c)

    for d in range(1, col_count):
        source = lax.rem(col + d, col_count)
        pltpu.make_async_remote_copy(
            src_ref=own_ref.at[source], dst_ref=own_ref.at[source], send_sem=own_send.at[d],
            recv_sem=own_recv.at[source], device_id=(row, source), device_id_type=MESH,
        ).wait_recv()
    twin_copy.wait_send()
    for copy in started:
        copy.wait_send()
    if direct:
        @pl.when(ends)
        def _():
            y_sum(1).wait_send()
    else:
        for d in range(1, ny):
            y_sum(d).wait_send()
    events(True)
    keep_own.wait()
    pltpu.make_async_copy(piece, slot(row, col), local_sem.at[1]).wait()


def gather(mock_maps, window_blocks, row_count, col_count):
    mocks = mock_maps.shape[0]
    width = mock_maps.shape[1] // col_count
    part = WINDOW * width // row_count
    ny = row_count // CORES
    nx = col_count // ALONG_Z
    dma = pltpu.SemaphoreType.DMA
    shares = 1 if part == width else ny
    return pl.pallas_call(
        functools.partial(gather_kernel, row_count, col_count),
        out_shape=(
            jax.ShapeDtypeStruct((col_count, mocks, width), jnp.bfloat16),
            jax.ShapeDtypeStruct((row_count, col_count, mocks, part), jnp.bfloat16),
        ),
        in_specs=[pl.BlockSpec(memory_space=pltpu.SMEM), pl.BlockSpec(memory_space=pl.ANY)],
        out_specs=(pl.BlockSpec(memory_space=pl.ANY), pl.BlockSpec(memory_space=pl.ANY)),
        scratch_shapes=[
            pltpu.VMEM(mock_maps.shape, jnp.bfloat16),
            pltpu.VMEM((shares, mocks, part), jnp.bfloat16),
            pltpu.VMEM((shares, mocks, part), jnp.bfloat16),
            pltpu.VMEM((shares, mocks, part), jnp.bfloat16),
            pltpu.VMEM((ny, mocks, part), jnp.bfloat16),
            pltpu.VMEM((ny, mocks, part), jnp.bfloat16),
            pltpu.VMEM((mocks, part), jnp.bfloat16),
            dma, dma, dma((ny,)), dma((ny,)),
            dma((2, ALONG_Z)), dma((nx, ALONG_Z)), dma((ny, col_count)),
            dma((row_count, col_count)), dma((row_count, col_count)),
            dma((col_count,)), dma((col_count,)), dma((3,)),
        ],
        compiler_params=pltpu.CompilerParams(
            collective_id=0, has_side_effects=True, vmem_limit_bytes=60 * 2**20
        ),
        name="gather",
    )(window_blocks, mock_maps)


def ordered_slot(window_ref, last, slot):
    block = window_ref[slot]
    rank = jnp.int32(1)
    for t in range(WINDOW):
        middle = (t < slot) & (window_ref[t] != 0) & (window_ref[t] != last)
        rank = rank + middle.astype(jnp.int32)
    return jnp.where(block == 0, 0, jnp.where(block == last, WINDOW - 1, rank))


ONES = 16
HALVES = 2


def tile_kernel(
    parts, last, window_hbm, kept_hbm, index_hbm, table_hbm, own_hbm, panels_hbm, out_ref,
    window_ref, kept_ref, index_ref, table_ref, own_ref, panels_ref, own_t, own_sum, small_sem, own_sem, panel_sem,
):
    step, half = pl.program_id(0), pl.program_id(1)
    slot = step // parts
    count, width = own_ref.shape
    rows = width // HALVES
    steps = panels_ref.shape[0]

    def fetch(i):
        entry = ordered_slot(window_ref, last, i // parts) * parts + i % parts
        return pltpu.make_async_copy(panels_hbm.at[entry], panels_ref.at[i], panel_sem.at[i])

    @pl.when((step == 0) & (half == 0))
    def _():
        small = ((window_hbm, window_ref), (kept_hbm, kept_ref), (index_hbm, index_ref), (table_hbm, table_ref))
        copies = [pltpu.make_async_copy(src, dst, small_sem.at[i]) for i, (src, dst) in enumerate(small)]
        load_own = pltpu.make_async_copy(own_hbm, own_ref, own_sem)
        for copy in copies:
            copy.start()
        load_own.start()
        for copy in copies:
            copy.wait()
        for i in range(steps):
            @pl.when(kept_ref[0, i // parts] > 0)
            def _():
                fetch(i).start()
        load_own.wait()
        for h in range(HALVES):
            own_t[h, :ONES] = jnp.ones((ONES, count), jnp.bfloat16)
            own_t[h, ONES:] = own_ref[:, h * rows:(h + 1) * rows].T
            own_sum[h] = jnp.dot(
                own_t[h, ONES:], jnp.ones((count, 128), jnp.bfloat16), preferred_element_type=jnp.float32
            )

    kept = kept_ref[0, slot] > 0

    @pl.when(kept & (half == 0))
    def _():
        fetch(step).wait()

    @pl.when(kept)
    def _():
        scale = table_ref[index_ref[0, slot]] / (count - 1)
        panel = panels_ref[step]
        panel_mean = None
        for first in range(0, rows, rows // 2):
            skip = ONES if panel_mean is None else 0
            left = own_t[half, pl.ds(first + ONES - skip, rows // 2 + skip)]
            products = jnp.dot(left, panel, preferred_element_type=jnp.float32)
            if panel_mean is None:
                panel_mean = products[:1] * (scale / count)
            sums = own_sum[half, pl.ds(first, rows // 2)]
            for part in range(0, panel.shape[1], 128):
                here = slice(part, part + 128)
                value = scale * products[skip:, here] - sums * panel_mean[:, here]
                out_ref[first:first + rows // 2, here] = value.astype(jnp.bfloat16)

    @pl.when(jnp.logical_not(kept))
    def _():
        out_ref[...] = jnp.zeros_like(out_ref)


def tiles(own, panels, window_blocks, kept_tiles, taper_index, taper_table, last):
    count, width = own.shape
    steps, _, part = panels.shape
    parts = width // part
    dma = pltpu.SemaphoreType.DMA
    return pl.pallas_call(
        functools.partial(tile_kernel, parts, last),
        out_shape=jax.ShapeDtypeStruct((width, steps * part), jnp.bfloat16),
        grid=(steps, HALVES),
        in_specs=[pl.BlockSpec(memory_space=pl.ANY)] * 6,
        out_specs=pl.BlockSpec((width // HALVES, part), lambda i, h: (h, i)),
        scratch_shapes=[
            pltpu.SMEM(window_blocks.shape, jnp.int32),
            pltpu.SMEM(kept_tiles.shape, jnp.int32),
            pltpu.SMEM(taper_index.shape, jnp.int32),
            pltpu.SMEM(taper_table.shape, jnp.float32),
            pltpu.VMEM(own.shape, jnp.bfloat16),
            pltpu.VMEM(panels.shape, jnp.bfloat16),
            pltpu.VMEM((HALVES, ONES + width // HALVES, count), jnp.bfloat16),
            pltpu.VMEM((HALVES, width // HALVES, 128), jnp.float32),
            dma((4,)), dma, dma((steps,)),
        ],
        compiler_params=pltpu.CompilerParams(
            dimension_semantics=("arbitrary", "arbitrary"), vmem_limit_bytes=60 * 2**20
        ),
        name="tiles",
    )(window_blocks, kept_tiles, taper_index, taper_table, own, panels)


def per_device(row_count, col_count, mock_maps, window_blocks, kept_tiles, taper_index, taper_table):
    own, panels = gather(mock_maps, window_blocks, row_count, col_count)
    own = own.reshape(-1, own.shape[-1])
    panels = panels.reshape(panels.shape[0], -1, panels.shape[-1])
    last = row_count * col_count - 1
    return tiles(own, panels, window_blocks, kept_tiles, taper_index, taper_table, last)


def solution(mesh):
    in_specs = (P("col", "row"), P(), P(("row", "col"), None), P(("row", "col"), None), P())
    out_specs = P(("row", "col"), None)
    return jax.shard_map(
        functools.partial(per_device, mesh.shape["row"], mesh.shape["col"]),
        mesh=mesh, in_specs=in_specs, out_specs=out_specs, check_vma=False,
    )
```

```python
import functools

import jax
import jax.numpy as jnp
from jax import lax
from jax.experimental import pallas as pl
from jax.experimental.pallas import tpu as pltpu
from jax.sharding import PartitionSpec as P

MESH = pl.DeviceIdType.MESH
WINDOW = 4
CORES = 2
ALONG_Z = 4


def gather_kernel(
    row_count, col_count, window_ref, maps_ref, own_ref, panels_ref,
    maps, for_twin, mine, from_twin, summed, from_y, piece,
    twin_send, twin_recv, ysum_send, ysum_recv,
    z_send, x_send, y_send, core_send, panel_recv,
    own_send, own_recv, local_sem,
):
    ny, nx, nz = row_count // CORES, col_count // ALONG_Z, ALONG_Z
    row, col = lax.axis_index("row"), lax.axis_index("col")
    y, core = row // CORES, row % CORES
    z, x = col // nx, col % nx
    twin = y * CORES + (1 - core)
    width = own_ref.shape[2]
    part = panels_ref.shape[3]

    load_maps = pltpu.make_async_copy(maps_ref, maps, local_sem.at[2])
    load_maps.start()

    def row_of(d):
        return lax.rem(y + d, ny) * CORES + core

    barrier = pltpu.get_barrier_semaphore()
    peers = [(row, lax.rem(col + d, col_count)) for d in range(1, col_count)]
    peers += [(twin, col)] + [(row_of(d), col) for d in range(1, ny)]
    for peer in peers:
        pl.semaphore_signal(barrier, inc=1, device_id=peer, device_id_type=MESH)

    last = row_count * col_count - 1
    is_middle, rank, seen = [], [], 0
    for t in range(WINDOW):
        block = window_ref[t]
        is_middle.append(jnp.minimum(block, 1) * jnp.minimum(last - block, 1))
        rank.append(seen)
        seen = seen + is_middle[t]

    def masked(slot, offset):
        block = jnp.int32(0)
        for t in range(WINDOW):
            chosen = is_middle[t] * (1 - jnp.minimum(jnp.abs(rank[t] + 1 - slot), 1))
            block = block + chosen * window_ref[t]
        block = block + last * (1 - jnp.minimum(jnp.abs(slot - (WINDOW - 1)), 1))
        found = jnp.zeros((maps.shape[0], part), jnp.float32)
        for j in range(col_count):
            here = 1 - jnp.minimum(jnp.abs(block - (row * col_count + j)), 1)
            columns = maps[:, pl.ds(pl.multiple_of(j * width + offset, 128), part)]
            found = found + columns.astype(jnp.float32) * here.astype(jnp.float32)
        return found.astype(jnp.bfloat16)

    direct = part == width and row_count == WINDOW
    load_maps.wait()
    if direct:
        for_twin[0] = masked(1 + core, 0)
        mine[0] = masked(2 - core, 0)

    pl.semaphore_wait(barrier, len(peers))

    started = []

    def send(src, dst, send_sem, recv_sem, device):
        copy = pltpu.make_async_remote_copy(
            src_ref=src, dst_ref=dst, send_sem=send_sem, recv_sem=recv_sem,
            device_id=device, device_id_type=MESH,
        )
        copy.start()
        return copy

    def send_own(d):
        dest = lax.rem(col + d, col_count)
        columns = pl.ds(pl.multiple_of(dest * width, 128), width)
        started.append(send(
            maps_ref.at[:, columns], own_ref.at[col],
            own_send.at[d], own_recv.at[col], (row, dest),
        ))

    pending = sorted(
        range(1, col_count),
        key=lambda d: (1, abs(d - col_count // 2)) if d % nx else (0, -abs(d - col_count // 2)),
    )
    along_z = sum(d % nx == 0 for d in pending)

    def send_some(count):
        for _ in range(min(count, len(pending))):
            send_own(pending.pop(0))

    def slot(r, c):
        return panels_ref.at[r, c]

    def arrived(r, c):
        pltpu.make_async_remote_copy(
            src_ref=slot(r, c), dst_ref=slot(r, c), send_sem=core_send.at[r, c],
            recv_sem=panel_recv.at[r, c], device_id=(row, col), device_id_type=MESH,
        ).wait_recv()

    def out(src, r, c, send_sem, device, waiting):
        copy = pltpu.make_async_remote_copy(
            src_ref=src, dst_ref=slot(r, c), send_sem=send_sem,
            recv_sem=panel_recv.at[r, c], device_id=device, device_id_type=MESH,
        )
        if waiting:
            copy.wait_send()
        else:
            copy.start()

    def z_out(src, zz, up, waiting):
        to = z + 1 if up else z - 1

        @pl.when(to < nz if up else to >= 0)
        def _():
            c = zz * nx + x
            out(src, row, c, z_send.at[int(up), zz], (row, to * nx + x), waiting)

    def x_out(src, zz, waiting):
        c = zz * nx + x
        for d in range(1, nx):
            out(src, row, c, x_send.at[d, zz], (row, z * nx + lax.rem(x + d, nx)), waiting)

    def y_out(src, c, waiting):
        for d in range(1, ny):
            out(src, row, c, y_send.at[d, c], (row_of(d), col), waiting)

    def core_out(src, r, c, waiting):
        out(src, r, c, core_send.at[r, c], (twin, col), waiting)

    def at_z(d, body):
        if d == 0:
            body(z, None)
            return

        @pl.when(z >= d)
        def _():
            body(z - d, True)

        @pl.when(z + d < nz)
        def _():
            body(z + d, False)

    def own_event(src, waiting, along_y=True):
        z_out(src, z, True, waiting)
        z_out(src, z, False, waiting)
        if along_y:
            y_out(src, col, waiting)
        x_out(src, z, waiting)
        core_out(src, row, col, waiting)

    def z_event(waiting, zz, up):
        c = zz * nx + x
        src = slot(row, c)
        if not waiting:
            arrived(row, c)
        z_out(src, zz, up, waiting)
        y_out(src, c, waiting)
        x_out(src, zz, waiting)
        core_out(src, row, c, waiting)

    def x_event(waiting, zz, up):
        for d in range(1, nx):
            c = zz * nx + lax.rem(x + d, nx)
            if not waiting:
                arrived(row, c)
            y_out(slot(row, c), c, waiting)
            core_out(slot(row, c), row, c, waiting)

    def y_event(waiting, own_x, zz, up):
        for dx in ([0] if own_x else range(1, nx)):
            c = zz * nx + lax.rem(x + dx, nx)
            for d in range(1, ny):
                r = row_of(d)
                if not waiting:
                    arrived(r, c)
                core_out(slot(r, c), r, c, waiting)

    def events(waiting):
        if waiting:
            own_event(piece, True)
        for d in range(1, nz):
            at_z(d, functools.partial(z_event, waiting))
            if d == nz - 2 and not waiting:
                send_some(along_z - (2 if direct else 1))
            at_z(d - 1, functools.partial(x_event, waiting))
            if d >= nz - 2 and not waiting:
                send_some(len(pending) // 2 if d == nz - 2 else col_count)
        at_z(nz - 1, functools.partial(x_event, waiting))
        for d in range(nz):
            at_z(d, functools.partial(y_event, waiting, True))
            at_z(d, functools.partial(y_event, waiting, False))

    keep_own = pltpu.make_async_copy(
        maps_ref.at[:, pl.ds(pl.multiple_of(col * width, 128), width)], own_ref.at[col], local_sem.at[0]
    )
    keep_own.start()
    ends = lax.rem(row, row_count - 1) == 0

    def y_sum(d):
        return pltpu.make_async_remote_copy(
            src_ref=summed.at[d], dst_ref=from_y.at[ny - d], send_sem=ysum_send.at[d],
            recv_sem=ysum_recv.at[ny - d], device_id=(row_of(d), col), device_id_type=MESH,
        )

    if direct:
        first = pl.multiple_of((row // (row_count - 1)) * ((col_count - 1) * width), 128)
        held_piece = maps_ref.at[:, pl.ds(first, width)]

        twin_copy = send(for_twin, from_twin, twin_send, twin_recv, (twin, col))

        @pl.when(ends)
        def _():
            own_event(held_piece, False, along_y=False)
            pltpu.make_async_copy(held_piece, slot(row, col), local_sem.at[1]).start()

        twin_copy.wait_recv()
        summed[1] = mine[0] + from_twin[0]

        @pl.when(ends)
        def _():
            y_sum(1).start()
            y_out(held_piece, col, False)

        send_some(1)

        @pl.when(jnp.logical_not(ends))
        def _():
            y_sum(1).wait_recv()
            piece[...] = summed[1] + from_y[1]
            own_event(piece, False)
            pltpu.make_async_copy(piece, slot(row, col), local_sem.at[1]).start()
    else:
        for d in range(ny):
            for k, held in ((1 - core, for_twin), (core, mine)):
                first = (lax.rem(y + d, ny) * CORES + k) * part
                held[d] = masked(first // width, lax.rem(first, width))
        twin_copy = send(for_twin, from_twin, twin_send, twin_recv, (twin, col))
        twin_copy.wait_recv()
        for d in range(ny):
            summed[d] = mine[d] + from_twin[d]
        for d in range(1, ny):
            y_sum(d).start()
        total = summed[0]
        for d in range(1, ny):
            y_sum(d).wait_recv()
            total = total + from_y[ny - d]
        piece[...] = total
        own_event(piece, False)
        pltpu.make_async_copy(piece, slot(row, col), local_sem.at[1]).start()
    send_some(1)
    events(False)

    for d in range(ny):
        r = lax.rem(y + d, ny) * CORES + (1 - core)

        @pl.loop(0, col_count)
        def _(c):
            arrived(r, c)

    for d in range(1, col_count):
        source = lax.rem(col + d, col_count)
        pltpu.make_async_remote_copy(
            src_ref=own_ref.at[source], dst_ref=own_ref.at[source], send_sem=own_send.at[d],
            recv_sem=own_recv.at[source], device_id=(row, source), device_id_type=MESH,
        ).wait_recv()
    twin_copy.wait_send()
    for copy in started:
        copy.wait_send()
    if direct:
        @pl.when(ends)
        def _():
            y_sum(1).wait_send()
    else:
        for d in range(1, ny):
            y_sum(d).wait_send()
    events(True)
    keep_own.wait()
    pltpu.make_async_copy(piece, slot(row, col), local_sem.at[1]).wait()


def gather(mock_maps, window_blocks, row_count, col_count):
    mocks = mock_maps.shape[0]
    width = mock_maps.shape[1] // col_count
    part = WINDOW * width // row_count
    ny = row_count // CORES
    nx = col_count // ALONG_Z
    dma = pltpu.SemaphoreType.DMA
    shares = 1 if part == width else ny
    return pl.pallas_call(
        functools.partial(gather_kernel, row_count, col_count),
        out_shape=(
            jax.ShapeDtypeStruct((col_count, mocks, width), jnp.bfloat16),
            jax.ShapeDtypeStruct((row_count, col_count, mocks, part), jnp.bfloat16),
        ),
        in_specs=[pl.BlockSpec(memory_space=pltpu.SMEM), pl.BlockSpec(memory_space=pl.ANY)],
        out_specs=(pl.BlockSpec(memory_space=pl.ANY), pl.BlockSpec(memory_space=pl.ANY)),
        scratch_shapes=[
            pltpu.VMEM(mock_maps.shape, jnp.bfloat16),
            pltpu.VMEM((shares, mocks, part), jnp.bfloat16),
            pltpu.VMEM((shares, mocks, part), jnp.bfloat16),
            pltpu.VMEM((shares, mocks, part), jnp.bfloat16),
            pltpu.VMEM((ny, mocks, part), jnp.bfloat16),
            pltpu.VMEM((ny, mocks, part), jnp.bfloat16),
            pltpu.VMEM((mocks, part), jnp.bfloat16),
            dma, dma, dma((ny,)), dma((ny,)),
            dma((2, ALONG_Z)), dma((nx, ALONG_Z)), dma((ny, col_count)),
            dma((row_count, col_count)), dma((row_count, col_count)),
            dma((col_count,)), dma((col_count,)), dma((3,)),
        ],
        compiler_params=pltpu.CompilerParams(
            collective_id=0, has_side_effects=True, vmem_limit_bytes=60 * 2**20
        ),
        name="gather",
    )(window_blocks, mock_maps)


def ordered_slot(window_ref, last, slot):
    block = window_ref[slot]
    rank = jnp.int32(1)
    for t in range(WINDOW):
        middle = (t < slot) & (window_ref[t] != 0) & (window_ref[t] != last)
        rank = rank + middle.astype(jnp.int32)
    return jnp.where(block == 0, 0, jnp.where(block == last, WINDOW - 1, rank))


ONES = 16
HALVES = 2


def tile_kernel(
    parts, last, window_hbm, kept_hbm, index_hbm, table_hbm, own_hbm, panels_hbm, out_ref,
    window_ref, kept_ref, index_ref, table_ref, own_ref, panels_ref, own_t, own_sum, small_sem, own_sem, panel_sem,
):
    step, half = pl.program_id(0), pl.program_id(1)
    slot = step // parts
    count, width = own_ref.shape
    rows = width // HALVES
    steps = panels_ref.shape[0]

    def fetch(i):
        entry = ordered_slot(window_ref, last, i // parts) * parts + i % parts
        return pltpu.make_async_copy(panels_hbm.at[entry], panels_ref.at[i], panel_sem.at[i])

    @pl.when((step == 0) & (half == 0))
    def _():
        small = ((window_hbm, window_ref), (kept_hbm, kept_ref), (index_hbm, index_ref), (table_hbm, table_ref))
        copies = [pltpu.make_async_copy(src, dst, small_sem.at[i]) for i, (src, dst) in enumerate(small)]
        load_own = pltpu.make_async_copy(own_hbm, own_ref, own_sem)
        for copy in copies:
            copy.start()
        load_own.start()
        for copy in copies:
            copy.wait()
        for i in range(steps):
            @pl.when(kept_ref[0, i // parts] > 0)
            def _():
                fetch(i).start()
        load_own.wait()
        for h in range(HALVES):
            own_t[h, :ONES] = jnp.ones((ONES, count), jnp.bfloat16)
            own_t[h, ONES:] = own_ref[:, h * rows:(h + 1) * rows].T
            own_sum[h] = jnp.dot(
                own_t[h, ONES:], jnp.ones((count, 128), jnp.bfloat16), preferred_element_type=jnp.float32
            )

    kept = kept_ref[0, slot] > 0

    @pl.when(kept & (half == 0))
    def _():
        fetch(step).wait()

    @pl.when(kept)
    def _():
        scale = table_ref[index_ref[0, slot]] / (count - 1)
        panel = panels_ref[step]
        panel_mean = None
        for first in range(0, rows, rows):
            skip = ONES if panel_mean is None else 0
            left = own_t[half, pl.ds(first + ONES - skip, rows + skip)]
            products = jnp.dot(left, panel, preferred_element_type=jnp.float32)
            if panel_mean is None:
                panel_mean = products[:1] * (scale / count)
            sums = own_sum[half, pl.ds(first, rows)]
            for part in range(0, panel.shape[1], 128):
                here = slice(part, part + 128)
                value = scale * products[skip:, here] - sums * panel_mean[:, here]
                out_ref[first:first + rows, here] = value.astype(jnp.bfloat16)

    @pl.when(jnp.logical_not(kept))
    def _():
        out_ref[...] = jnp.zeros_like(out_ref)


def tiles(own, panels, window_blocks, kept_tiles, taper_index, taper_table, last):
    count, width = own.shape
    steps, _, part = panels.shape
    parts = width // part
    dma = pltpu.SemaphoreType.DMA
    return pl.pallas_call(
        functools.partial(tile_kernel, parts, last),
        out_shape=jax.ShapeDtypeStruct((width, steps * part), jnp.bfloat16),
        grid=(steps, HALVES),
        in_specs=[pl.BlockSpec(memory_space=pl.ANY)] * 6,
        out_specs=pl.BlockSpec((width // HALVES, part), lambda i, h: (h, i)),
        scratch_shapes=[
            pltpu.SMEM(window_blocks.shape, jnp.int32),
            pltpu.SMEM(kept_tiles.shape, jnp.int32),
            pltpu.SMEM(taper_index.shape, jnp.int32),
            pltpu.SMEM(taper_table.shape, jnp.float32),
            pltpu.VMEM(own.shape, jnp.bfloat16),
            pltpu.VMEM(panels.shape, jnp.bfloat16),
            pltpu.VMEM((HALVES, ONES + width // HALVES, count), jnp.bfloat16),
            pltpu.VMEM((HALVES, width // HALVES, 128), jnp.float32),
            dma((4,)), dma, dma((steps,)),
        ],
        compiler_params=pltpu.CompilerParams(
            dimension_semantics=("arbitrary", "arbitrary"), vmem_limit_bytes=60 * 2**20
        ),
        name="tiles",
    )(window_blocks, kept_tiles, taper_index, taper_table, own, panels)


def per_device(row_count, col_count, mock_maps, window_blocks, kept_tiles, taper_index, taper_table):
    own, panels = gather(mock_maps, window_blocks, row_count, col_count)
    own = own.reshape(-1, own.shape[-1])
    panels = panels.reshape(panels.shape[0], -1, panels.shape[-1])
    last = row_count * col_count - 1
    return tiles(own, panels, window_blocks, kept_tiles, taper_index, taper_table, last)


def solution(mesh):
    in_specs = (P("col", "row"), P(), P(("row", "col"), None), P(("row", "col"), None), P())
    out_specs = P(("row", "col"), None)
    return jax.shard_map(
        functools.partial(per_device, mesh.shape["row"], mesh.shape["col"]),
        mesh=mesh, in_specs=in_specs, out_specs=out_specs, check_vma=False,
    )
```
